128 devices in a mesh: dp: 4 (over y), ctx: 32 (over z, x, core).
Axes of the slice: x: 4, y: 4, z: 4, core: 2. Of those that a mesh axis runs over, the one named last changes fastest.
Arguments:
- tokens: bfloat16 [4, 20480, 4096], P('dp', 'ctx'), may hold values from -400 to 400
- w_query: bfloat16 [4096, 1024], P(('dp', 'ctx')), may hold values from -0.09375 to 0.09375
- w_key: bfloat16 [4096, 1024], P(('dp', 'ctx')), may hold values from -0.09375 to 0.09375
- w_value: bfloat16 [4096, 2048], P(('dp', 'ctx')), may hold values from -0.09375 to 0.09375
- w_gates: bfloat16 [4096, 8], P(('dp', 'ctx')), may hold values from -0.09375 to 0.09375
- forget_bias: float32 [4], replicated, may hold values from 2 to 15
- doc_lengths: int32 [4, 16], P('dp'), may hold values from 1 to 10240, 20480 in all within a row
Outputs:
- head_out: bfloat16 [4, 20480, 2048], P('dp', 'ctx')
The draws below stay inside these ranges and needn't reach their ends.
Inputs may be any that keep to these rules, and one draw needn't show every extreme that they name: `doc_lengths`: each sequence's 16 lengths sum to 20480; the longest is exactly 10240.
All inputs are finite; a program needn't handle non-finite values.
Results may differ from the reference program's by a relative error of at most 0.025.
Values may be sent and summed in bfloat16 or wider, within the bound.
No kernel may reach another device: no remote copies, remote signals or barrier semaphores. Data moves between devices by JAX's collectives and lax.ppermute only.
A program may use at most 128 MiB of HBM per device.

```python
import math
import jax
import jax.numpy as jnp
import numpy as np
from jax import lax

D = 4096
HEADS = 4
DQK = 256
DV = 512
TOK_DEV = 640
NDOC = 16
LEN = 20480
NSEQ = 4
N_CTX = 32


def draw_tokens(key, part):
    key = jax.random.fold_in(key, 11)
    k_base, k_rows, k_cols = jax.random.split(key, 3)
    spread = jnp.log(10.0)
    row_scale = jnp.exp(jax.random.uniform(k_rows, (NSEQ, LEN, 1), jnp.float32, 0.0, spread))
    col_scale = jnp.exp(jax.random.uniform(k_cols, (1, 1, D), jnp.float32, 0.0, spread))
    base = jnp.clip(jax.random.normal(k_base, (NSEQ, LEN, D), jnp.float32), -4.0, 4.0)
    return (base * row_scale * col_scale).astype(jnp.bfloat16)


def draw_forget_bias(key, part):
    key = jax.random.fold_in(key, 23)
    k_pick, k_slow, k_fast = jax.random.split(key, 3)
    share = 0.5
    pick = jax.random.uniform(k_pick, (HEADS,), jnp.float32)
    slow = (pick < share) | (pick == jnp.min(pick))
    slow_bias = jnp.log(jnp.float32(LEN)) + jax.random.uniform(k_slow, (HEADS,), jnp.float32, -0.7, 2.0)
    fast_bias = jax.random.uniform(k_fast, (HEADS,), jnp.float32, 2.0, 3.5)
    return jnp.where(slow, slow_bias, fast_bias).astype(jnp.float32)


def block_scale(rng, shape, cuts, least, top_value):
    gain, own = 1.0, jax.random.fold_in(rng, 6)
    for dim, blocks in cuts:
        steps = jnp.exp(jax.random.uniform(jax.random.fold_in(own, dim), (blocks,), jnp.float32, least / len(cuts), top_value / len(cuts)))
        gain = gain * jnp.repeat(steps, shape[dim] // blocks).reshape([-1 if axis == dim else 1 for axis in range(len(shape))])
    return gain


def length_profile(number_of, total, most, slope):
    portions = [(1 << 20) // math.isqrt(rank ** slope) + 1 for rank in range(2, number_of + 1)]
    surplus, given = total - most - (number_of - 1), [1] * (number_of - 1)
    while surplus > 0:
        candidates = [i for i in range(number_of - 1) if given[i] < most]
        mass, remaining = sum([portions[i] for i in candidates]), surplus
        for i in candidates:
            extra = min(most - given[i], max(1, remaining * portions[i] // mass), surplus)
            given[i] = given[i] + extra
            surplus = surplus - extra
    return np.array([most] + given)


def ragged_sizes(own_key, number_of, total, most, skew):
    if number_of == 2:
        one = jax.random.randint(own_key, (), max(1, total - most), min(most, total - 1) + 1)
        return jnp.stack([one, total - one])
    sizes = jnp.asarray(length_profile(number_of, total, most, skew), jnp.int32)
    twos = (number_of - 1) // 2
    source_of, receiver = sizes[1:1 + 2 * twos:2], sizes[2:2 + 2 * twos:2]
    slack = jnp.minimum(source_of - 1, most - receiver)
    shifted = jax.random.randint(jax.random.fold_in(own_key, 1), (twos,), 0, 1 << 20) % (slack + 1)
    sizes = sizes.at[1:1 + 2 * twos:2].set(source_of - shifted).at[2:2 + 2 * twos:2].set(receiver + shifted)
    return sizes[jax.random.permutation(jax.random.fold_in(own_key, 2), number_of)]


def noise(own_key, shape, scale, bound, pieces=(), held_as=jnp.bfloat16):
    drawn = scale * jax.random.normal(own_key, shape, jnp.float32)
    if pieces:
        drawn = drawn * block_scale(own_key, shape, pieces, -0.22, 0.18)
    return jnp.clip(drawn, -bound, bound).astype(held_as)


def setup_inputs(seed: int = 0) -> dict:
    arg_keys = jax.random.split(jax.random.key(seed), 8)
    return {
        "tokens": draw_tokens(jax.random.fold_in(arg_keys[7], 71), 0),
        "w_query": noise(arg_keys[1], (D, HEADS * DQK), D ** -0.5, 0.09375, ((0, 128),)),
        "w_key": noise(arg_keys[2], (D, HEADS * DQK), D ** -0.5, 0.09375, ((0, 128),)),
        "w_value": noise(arg_keys[3], (D, HEADS * DV), D ** -0.5, 0.09375, ((0, 128),)),
        "w_gates": noise(arg_keys[4], (D, 2 * HEADS), D ** -0.5, 0.09375, ((0, 128),)),
        "forget_bias": draw_forget_bias(jax.random.fold_in(arg_keys[7], 71), 0),
        "doc_lengths": jax.vmap(lambda own: ragged_sizes(own, NDOC, LEN, LEN // 2, 2))(jax.random.split(arg_keys[6], NSEQ)).reshape((NSEQ, NDOC)).astype(jnp.int32),
    }


def normalize(block):
    values = block.astype(jnp.float32)
    scale = lax.rsqrt(lax.optimization_barrier(jnp.mean(values * values, axis=-1, keepdims=True)) + 1e-06)
    return (values * scale).astype(jnp.bfloat16)

def gate_terms(gates, forget_bias, resets):
    heads = forget_bias.shape[0]
    in_gate = gates[:, :heads]
    log_forget = jax.nn.log_sigmoid(gates[:, heads:] + forget_bias[None, :])
    cumul = jnp.cumsum(log_forget, axis=0)
    segment = jnp.cumsum(resets.astype(jnp.int32))
    return (in_gate, cumul, segment)

def shard_state(keys, values, in_gate, cumul, segment):
    rows = keys.shape[0]
    heads = in_gate.shape[1]
    keys3 = keys.reshape(rows, heads, -1)
    value_rows3 = values.reshape(rows, heads, -1)
    last = cumul[-1]
    same = (segment == segment[-1])[:, None]
    weight = jnp.exp(jnp.where(same, last[None, :] - cumul + in_gate, -1e+30))
    scaled_values = (keys3.astype(jnp.float32) * weight[:, :, None]).astype(jnp.bfloat16)
    memory_state = jnp.einsum('bdy,bdr->dyr', scaled_values.astype(jnp.float32), value_rows3.astype(jnp.float32))
    decay = jnp.exp(last) * (segment[-1] == 0).astype(jnp.float32)
    return (decay.astype(jnp.bfloat16), memory_state.astype(jnp.bfloat16))

def shard_output(queries, keys, values, in_gate, cumul, segment, carried_state):
    rows = queries.shape[0]
    heads = in_gate.shape[1]
    query_rows3 = queries.reshape(rows, heads, -1).astype(jnp.float32)
    keys3 = keys.reshape(rows, heads, -1).astype(jnp.float32)
    value_rows3 = values.reshape(rows, heads, -1).astype(jnp.float32)
    decay_factor = 1.0 / jnp.sqrt(jnp.float32(query_rows3.shape[2]))
    scores = jnp.einsum('thk,shk->hts', query_rows3, keys3) * decay_factor
    order = jnp.arange(rows, dtype=jnp.int32)
    mask = (order[:, None] >= order[None, :]) & (segment[:, None] == segment[None, :])
    diff = cumul.T[:, :, None] - cumul.T[:, None, :] + in_gate.T[:, None, :]
    mixed = (scores * jnp.exp(jnp.where(mask[None], diff, -1e+30))).astype(jnp.bfloat16)
    intra = jnp.einsum('hts,shv->thv', mixed.astype(jnp.float32), value_rows3)
    decay_reach = jnp.exp(cumul) * (segment == 0).astype(jnp.float32)[:, None]
    between_shards = jnp.einsum('wia,iax->wix', query_rows3, carried_state.astype(jnp.float32)) * (decay_reach * decay_factor)[:, :, None]
    readout = intra + between_shards
    scale = lax.rsqrt(lax.optimization_barrier(jnp.mean(readout * readout, axis=-1, keepdims=True)) + 1e-05)
    return (readout * scale).astype(jnp.bfloat16).reshape(rows, -1)

def reference(tokens, w_query, w_key, w_value, w_gates, forget_bias, doc_lengths):

    def one_sequence(items):
        sequence, lengths = items
        starts = jnp.cumsum(lengths) - lengths
        shards = sequence.reshape(N_CTX, TOK_DEV, D)
        offsets = jnp.arange(N_CTX, dtype=jnp.int32) * TOK_DEV

        def step(carried_state, shard_items):
            block, offset = shard_items
            normed = normalize(block)
            queries = jnp.dot(normed, w_query, preferred_element_type=jnp.float32).astype(jnp.bfloat16)
            keys = jnp.dot(normed, w_key, preferred_element_type=jnp.float32).astype(jnp.bfloat16)
            values = jnp.dot(normed, w_value, preferred_element_type=jnp.float32).astype(jnp.bfloat16)
            gates = jnp.dot(normed, w_gates, preferred_element_type=jnp.float32)
            positions = offset + jnp.arange(TOK_DEV, dtype=jnp.int32)
            resets = jnp.any(positions[:, None] == starts[None, :].astype(jnp.int32), axis=1)
            in_gate, cumul, segment = gate_terms(gates, forget_bias, resets)
            decay, memory_state = shard_state(keys, values, in_gate, cumul, segment)
            out = shard_output(queries, keys, values, in_gate, cumul, segment, carried_state)
            decay_f = lax.optimization_barrier(decay).astype(jnp.float32)
            fresh = (decay_f[:, None, None] * carried_state.astype(jnp.float32) + memory_state.astype(jnp.float32)).astype(jnp.bfloat16)
            return (fresh, out)
        start_state = jnp.zeros((HEADS, DQK, DV), jnp.bfloat16)
        _, outs = lax.scan(step, start_state, (shards, offsets))
        return outs.reshape(LEN, HEADS * DV)
    return lax.map(one_sequence, (tokens, doc_lengths))
```

```python
import functools

import jax
import jax.numpy as jnp
from jax import lax
from jax.experimental import pallas as pl
from jax.experimental.pallas import tpu as pltpu
from jax.sharding import Mesh, PartitionSpec as P

ROWS = 640
DQK = 256
DV = 512
BF = jnp.bfloat16
F32 = jnp.float32
VMEM_LIMIT = 48 * 1024 * 1024


def swap(value):
    return lax.ppermute(value, "core", [(0, 1), (1, 0)])


def shift(value, axis, by):
    return lax.ppermute(value, axis, [(i, (i + by) % 4) for i in range(4)])


def normalize(block):
    values = block.astype(F32)
    scale = lax.rsqrt(jnp.mean(values * values, axis=-1, keepdims=True) + 1e-06)
    return (values * scale).astype(BF)


def state_kernel(cols_ref, key_ref, value_ref, out_ref):
    head = pl.program_id(1)
    weight = jnp.where(head == 0, cols_ref[0, :, 4:5], cols_ref[0, :, 5:6])
    scaled = (key_ref[...].astype(F32) * weight).astype(BF)
    out_ref[0, 0] = lax.dot_general(
        scaled, value_ref[...], (((0,), (0,)), ((), ())), preferred_element_type=F32
    ).astype(BF)


def states(cols, qkv):
    return pl.pallas_call(
        state_kernel,
        grid=(2, 2),
        in_specs=[
            pl.BlockSpec((1, ROWS, 8), lambda s, h: (s, 0, 0)),
            pl.BlockSpec((ROWS, DQK), lambda s, h: (s, 2 + h)),
            pl.BlockSpec((ROWS, DV), lambda s, h: (s, 2 + h)),
        ],
        out_specs=pl.BlockSpec((1, 1, DQK, DV), lambda s, h: (s, h, 0, 0)),
        out_shape=jax.ShapeDtypeStruct((2, 2, DQK, DV), BF),
        compiler_params=pltpu.CompilerParams(vmem_limit_bytes=VMEM_LIMIT),
        cost_estimate=pl.CostEstimate(
            flops=4 * 2 * ROWS * DQK * DV, bytes_accessed=5 << 20, transcendentals=0
        ),
        name="states",
    )(cols, qkv, qkv)


def intra_kernel(cols_ref, rows_ref, query_ref, key_ref, value_ref, out_ref):
    head = pl.program_id(1)
    cumul = jnp.where(head == 0, cols_ref[0, :, 0:1], cols_ref[0, :, 1:2])
    segment = cols_ref[0, :, 6:7]
    cumul_row = jnp.where(head == 0, rows_ref[0, 0:1, :], rows_ref[0, 1:2, :])
    gate_row = jnp.where(head == 0, rows_ref[0, 2:3, :], rows_ref[0, 3:4, :])
    segment_row = rows_ref[0, 4:5, :]
    for start, size in ((0, 256), (256, 384)):
        reach = start + size
        scores = lax.dot_general(
            query_ref[start:reach, :],
            key_ref[:reach, :],
            (((1,), (1,)), ((), ())),
            preferred_element_type=F32,
        ) * (DQK**-0.5)
        later = start + lax.broadcasted_iota(jnp.int32, (size, reach), 0)
        earlier = lax.broadcasted_iota(jnp.int32, (size, reach), 1)
        keep = (later >= earlier) & (segment[start:reach] == segment_row[:, :reach])
        diff = cumul[start:reach] - cumul_row[:, :reach] + gate_row[:, :reach]
        mixed = (scores * jnp.exp(jnp.where(keep, diff, -1e30))).astype(BF)
        out_ref[start:reach, :] = jnp.dot(
            mixed, value_ref[:reach, :], preferred_element_type=F32
        )


def intra(cols, rows, qkv):
    return pl.pallas_call(
        intra_kernel,
        grid=(2, 2),
        in_specs=[
            pl.BlockSpec((1, ROWS, 8), lambda s, h: (s, 0, 0)),
            pl.BlockSpec((1, 8, ROWS), lambda s, h: (s, 0, 0)),
            pl.BlockSpec((ROWS, DQK), lambda s, h: (s, h)),
            pl.BlockSpec((ROWS, DQK), lambda s, h: (s, 2 + h)),
            pl.BlockSpec((ROWS, DV), lambda s, h: (s, 2 + h)),
        ],
        out_specs=pl.BlockSpec((ROWS, DV), lambda s, h: (s, h)),
        out_shape=jax.ShapeDtypeStruct((2 * ROWS, 2 * DV), F32),
        compiler_params=pltpu.CompilerParams(vmem_limit_bytes=VMEM_LIMIT),
        cost_estimate=pl.CostEstimate(
            flops=4 * 2 * ROWS * ROWS * (DQK + DV),
            bytes_accessed=12 << 20,
            transcendentals=4 * ROWS * ROWS,
        ),
        name="intra",
    )(cols, rows, qkv, qkv, qkv)


def readout_kernel(cols_ref, query_ref, intra_ref, carried_ref, out_ref):
    head = pl.program_id(0)
    reach = jnp.where(head == 0, cols_ref[0, :, 2:3], cols_ref[0, :, 3:4])
    between = jnp.dot(query_ref[...], carried_ref[0], preferred_element_type=F32) * reach
    readout = intra_ref[...] + between
    scale = lax.rsqrt(jnp.mean(readout * readout, axis=-1, keepdims=True) + 1e-05)
    out_ref[...] = (readout * scale).astype(BF)


def readout(slot, cols, qkv, inner, carried):
    return pl.pallas_call(
        readout_kernel,
        grid=(2,),
        in_specs=[
            pl.BlockSpec((1, ROWS, 8), lambda h: (slot, 0, 0)),
            pl.BlockSpec((ROWS, DQK), lambda h: (slot, h)),
            pl.BlockSpec((ROWS, DV), lambda h: (slot, h)),
            pl.BlockSpec((1, DQK, DV), lambda h: (h, 0, 0)),
        ],
        out_specs=pl.BlockSpec((ROWS, DV), lambda h: (0, h)),
        out_shape=jax.ShapeDtypeStruct((ROWS, 2 * DV), BF),
        compiler_params=pltpu.CompilerParams(vmem_limit_bytes=VMEM_LIMIT),
        cost_estimate=pl.CostEstimate(
            flops=2 * 2 * ROWS * DQK * DV, bytes_accessed=5 << 20, transcendentals=0
        ),
        name="readout",
    )(cols, qkv, inner, carried)


def join(decay, earlier, later):
    return (decay.astype(F32)[:, None, None] * earlier.astype(F32) + later.astype(F32)).astype(BF)


def times(left, right):
    return (left.astype(F32) * right.astype(F32)).astype(BF)


def pack(state, decay):
    tail = jnp.broadcast_to(decay[:, None, None], (2, 8, DV))
    return jnp.concatenate([state, tail], axis=1)


def unpack(message):
    return message[:, :-8], message[:, -1, 0]


def in_order(mine, axis, send):
    place = lax.axis_index(axis)
    blocks = [mine] + [shift(send(by), axis, by) for by in (1, 2, 3)]
    stacked = jnp.stack(blocks)
    return [lax.dynamic_index_in_dim(stacked, (place - j) % 4, 0, False) for j in range(4)]


def carry_in(decay, state):
    x, z = lax.axis_index("x"), lax.axis_index("z")
    quarters = state.reshape(2, 4, DQK // 4, DV)

    def piece(by):
        return pack(lax.dynamic_index_in_dim(quarters, (x + by) % 4, 1, False), decay)

    line = [unpack(block) for block in in_order(piece(0), "x", piece)]
    prior = jnp.zeros_like(line[0][0])
    reach = jnp.ones_like(decay)
    priors, reaches = [], []
    for block, fade in line:
        priors.append(prior)
        reaches.append(reach)
        prior = join(fade, prior, block)
        reach = times(fade, reach)
    whole = pack(prior, reach)
    before = jnp.zeros_like(prior)
    for j, message in enumerate(in_order(whole, "z", lambda by: whole)):
        block, fade = unpack(message)
        before = jnp.where(j < z, join(fade, before, block), before)
    backs = jnp.stack([join(reaches[j], before, priors[j]) for j in range(4)])

    def back(by):
        return lax.dynamic_index_in_dim(backs, (x + by) % 4, 0, False)

    return jnp.stack(in_order(back(0), "x", back), axis=1).reshape(2, DQK, DV)


def per_device(tokens, w_query, w_key, w_value, w_gates, forget_bias, doc_lengths):
    core = lax.axis_index("core")
    chip = lax.axis_index("z") * 4 + lax.axis_index("x")

    def columns(which):
        def part(weight):
            width = weight.shape[1] // 2
            return lax.dynamic_slice_in_dim(weight, which * width, width, 1)

        gates = w_gates.reshape(-1, 2, 2, 2)
        gates = lax.dynamic_index_in_dim(gates, which, 2, False).reshape(-1, 4)
        gates = jnp.pad(gates, ((0, 0), (0, 124)))
        return jnp.concatenate([part(w_query), part(w_key), part(w_value), gates], axis=1)

    mine, theirs = columns(core), swap(columns(1 - core))
    block = jnp.where(
        core == 0,
        jnp.concatenate([mine, theirs], axis=0),
        jnp.concatenate([theirs, mine], axis=0),
    )
    weights = lax.all_gather(block, ("y", "z", "x"), axis=0, tiled=True)

    normed = normalize(tokens[0])
    normed = jnp.concatenate([normed, swap(normed)], axis=0)
    qkv = jnp.dot(normed, weights[:, :2048], preferred_element_type=F32).astype(BF)
    gates = jnp.dot(normed, weights[:, 2048:], preferred_element_type=F32)

    gates = gates[:, :4].reshape(2, ROWS, 4)
    lengths = doc_lengths[0]
    starts = jnp.cumsum(lengths) - lengths
    shard = chip * 2 + jnp.stack([core, 1 - core])
    positions = shard[:, None] * ROWS + jnp.arange(ROWS, dtype=jnp.int32)[None, :]
    resets = jnp.any(positions[:, :, None] == starts[None, None, :], axis=-1)
    bias = lax.dynamic_slice_in_dim(forget_bias, core * 2, 2)
    in_gate = gates[:, :, :2]
    cumul = jnp.cumsum(jax.nn.log_sigmoid(gates[:, :, 2:] + bias), axis=1)
    segment = jnp.cumsum(resets.astype(jnp.int32), axis=1)
    last = cumul[:, -1]
    same = (segment == segment[:, -1:])[:, :, None]
    weight = jnp.exp(jnp.where(same, last[:, None, :] - cumul + in_gate, -1e30))
    decay = (jnp.exp(last) * (segment[:, -1:] == 0).astype(F32)).astype(BF)
    reach = jnp.exp(cumul) * (segment == 0).astype(F32)[:, :, None] * (DQK**-0.5)
    seg = segment.astype(F32)[:, :, None]
    cols = jnp.concatenate([cumul, reach, weight, seg, jnp.zeros_like(seg)], axis=2)
    rows = jnp.concatenate([cumul, in_gate, seg, jnp.zeros_like(seg), weight], axis=2)
    rows = rows.transpose(0, 2, 1)

    state = states(cols, qkv)
    first = lax.dynamic_index_in_dim(state, core, 0, False)
    second = lax.dynamic_index_in_dim(state, 1 - core, 0, False)
    fade_first = lax.dynamic_index_in_dim(decay, core, 0, False)
    fade_second = lax.dynamic_index_in_dim(decay, 1 - core, 0, False)
    carried = carry_in(times(fade_first, fade_second), join(fade_second, first, second))
    inner = intra(cols, rows, qkv)
    carried_second = join(fade_first, carried, first)
    own = jnp.where(core == 0, carried, carried_second)
    other = jnp.where(core == 0, carried_second, carried)
    outgoing = readout(1, cols, qkv, inner, other)
    incoming = swap(outgoing)
    kept = readout(0, cols, qkv, inner, own)
    result = jnp.where(
        core == 0,
        jnp.concatenate([kept, incoming], axis=1),
        jnp.concatenate([incoming, kept], axis=1),
    )
    return result.reshape(1, ROWS, 2048)


def solution(mesh):
    split = Mesh(mesh.devices.reshape(4, 4, 4, 2), ("y", "z", "x", "core"))
    weight_spec = P(("y", "z", "x", "core"), None)
    in_specs = (
        P("y", ("z", "x", "core"), None),
        weight_spec,
        weight_spec,
        weight_spec,
        weight_spec,
        P(),
        P("y", None),
    )
    out_specs = P("y", ("z", "x", "core"), None)
    return jax.shard_map(
        per_device, mesh=split, in_specs=in_specs, out_specs=out_specs, check_vma=False
    )
```

```python
import functools
import itertools

import jax
import jax.numpy as jnp
from jax import lax
from jax.experimental import pallas as pl
from jax.experimental.pallas import tpu as pltpu
from jax.sharding import Mesh, PartitionSpec as P

ROWS = 640
DQK = 256
DV = 512
OWN = 32
PIECE = 64
EXTRA = 16
WIDE = 512
BF = jnp.bfloat16
F32 = jnp.float32
COST = pl.CostEstimate(flops=0, bytes_accessed=1 << 10, transcendentals=0)
SMALL = pltpu.CompilerParams(vmem_limit_bytes=24 * 1024 * 1024)
PARAMS = pltpu.CompilerParams(vmem_limit_bytes=60 * 1024 * 1024)


def swap(value):
    return lax.ppermute(value, "core", [(0, 1), (1, 0)])


def shift(value, axis, by):
    return lax.ppermute(value, axis, [(i, (i + by) % 4) for i in range(4)])


def hop(value, axes, by):
    names, pairs = ("y", "z", "x", "core"), []
    for source in itertools.product(range(4), range(4), range(4), range(2)):
        target = list(source)
        at = names.index(axes[source[3]])
        target[at] = (target[at] + by) % 4
        flat = [((p[0] * 4 + p[1]) * 4 + p[2]) * 2 + p[3] for p in (source, target)]
        pairs.append(tuple(flat))
    return lax.ppermute(value, names, pairs)


def around(value, axes):
    return (value,) + tuple(hop(value, axes, by) for by in (3, 2, 1))


def places(at):
    return jnp.stack([at, (at + 1) % 4, (at + 2) % 4, (at + 3) % 4]).astype(jnp.int32)


def normalize_kernel(own_ref, mate_ref, out_ref):
    raw = jnp.where(pl.program_id(0) == 0, own_ref[...], mate_ref[...])
    values = raw.astype(F32)
    scale = lax.rsqrt(jnp.mean(values * values, axis=-1, keepdims=True) + 1e-06)
    out_ref[...] = (values * scale).astype(BF)


def normalize(own, mate):
    tile = 128
    steps = ROWS // tile
    return pl.pallas_call(
        normalize_kernel,
        grid=(2, steps),
        in_specs=[
            pl.BlockSpec((tile, 4096), lambda s, i: (jnp.where(s == 0, i, steps - 1), 0)),
            pl.BlockSpec((tile, 4096), lambda s, i: (jnp.where(s == 0, 0, i), 0)),
        ],
        out_specs=pl.BlockSpec((tile, 4096), lambda s, i: (s * steps + i, 0)),
        out_shape=jax.ShapeDtypeStruct((2 * ROWS, 4096), BF),
        compiler_params=PARAMS,
        cost_estimate=pl.CostEstimate(flops=0, bytes_accessed=21 << 20, transcendentals=0),
        name="normalize",
    )(own, mate)


def prepare_kernel(
    core_ref, query, key, value, mate_query, mate_key, mate_value, region, held_ref, rest_ref
):
    core = core_ref[0]
    narrow = pl.ds(pl.multiple_of(core * WIDE, WIDE), WIDE)
    wide = pl.ds(pl.multiple_of(core * 2 * WIDE, WIDE), 2 * WIDE)
    for source, rows in (((query, key, value), core), ((mate_query, mate_key, mate_value), 1 - core)):
        rows = pl.ds(pl.multiple_of(rows * OWN, OWN), OWN)
        held_ref[rows, :] = source[0][:, narrow]
        rest_ref[rows, :WIDE] = source[1][:, narrow]
        rest_ref[rows, WIDE:] = source[2][:, wide]
    held_ref[PIECE:, :] = region[...]


def prepare(core, own, mate, region):
    vmem = pl.BlockSpec(memory_space=pltpu.VMEM)
    return pl.pallas_call(
        prepare_kernel,
        in_specs=[pl.BlockSpec(memory_space=pltpu.SMEM)] + [vmem] * 7,
        out_specs=[vmem] * 2,
        out_shape=[
            jax.ShapeDtypeStruct((PIECE + EXTRA, WIDE), BF),
            jax.ShapeDtypeStruct((PIECE, 3 * WIDE), BF),
        ],
        compiler_params=PARAMS,
        cost_estimate=COST,
        name="prepare",
    )(core, *own, *mate, region)


def assemble_kernel(rows, final, places, *refs):
    blocks, out, held, regions, sems_in, sems_more, sems_out = refs[:4], refs[4:-5], *refs[-5:]
    loads, extras = [], []
    for which, block in enumerate(blocks):
        start = pl.multiple_of(places[which] * rows, PIECE)
        loads.append(
            pltpu.make_async_copy(
                block.at[pl.ds(0, rows), :], held.at[pl.ds(start, rows), :], sems_in.at[which]
            )
        )
        extras.append(
            pltpu.make_async_copy(
                block.at[pl.ds(rows, EXTRA), :], regions.at[which], sems_more.at[which]
            )
        )
    for copy in extras + loads:
        copy.start()
    for copy in extras:
        copy.wait()
    held[4 * rows :, :] = (regions[0] + regions[1]) + (regions[2] + regions[3])
    for copy in loads:
        copy.wait()
    if final:
        stores = [
            pltpu.make_async_copy(held.at[pl.ds(0, 4 * rows), :], out[0], sems_out.at[0]),
            pltpu.make_async_copy(held.at[pl.ds(4 * rows, EXTRA), :], out[1], sems_out.at[1]),
        ]
    else:
        stores = [pltpu.make_async_copy(held, out[0], sems_out.at[0])]
    for copy in stores:
        copy.start()
    for copy in stores:
        copy.wait()


def assemble(places, blocks, rows, final):
    hbm = pl.BlockSpec(memory_space=pl.ANY)
    if final:
        shapes = [(4 * rows, WIDE), (EXTRA, WIDE)]
    else:
        shapes = [(4 * rows + EXTRA, WIDE)]
    return pl.pallas_call(
        functools.partial(assemble_kernel, rows, final),
        in_specs=[pl.BlockSpec(memory_space=pltpu.SMEM)] + [hbm] * 4,
        out_specs=[hbm] * len(shapes),
        out_shape=[jax.ShapeDtypeStruct(shape, BF) for shape in shapes],
        scratch_shapes=[
            pltpu.VMEM((4 * rows + EXTRA, WIDE), BF),
            pltpu.VMEM((4, EXTRA, WIDE), BF),
            pltpu.SemaphoreType.DMA((4,)),
            pltpu.SemaphoreType.DMA((4,)),
            pltpu.SemaphoreType.DMA((2,)),
        ],
        compiler_params=PARAMS,
        cost_estimate=COST,
        name="assemble",
    )(places, *blocks)


def restore_kernel(places, *refs):
    blocks, out, held, sems_in, sem_out = refs[:4], *refs[4:]

    def run(target):
        copies = []
        for which, block in enumerate(blocks):
            for y in range(4):
                copies.append(
                    pltpu.make_async_copy(
                        block.at[:, y], target(y, places[which]), sems_in.at[4 * which + y]
                    )
                )
        for copy in copies:
            copy.start()
        for copy in copies:
            copy.wait()

    pl.when(places[4] == 0)(lambda: run(lambda y, x: held.at[y, :, x]))
    pl.when(places[4] == 1)(lambda: run(lambda y, z: held.at[y, z]))
    store = pltpu.make_async_copy(held, out, sem_out)
    store.start()
    store.wait()


def restore(places, blocks):
    hbm = pl.BlockSpec(memory_space=pl.ANY)
    shape = (4, 4, 4, PIECE, WIDE)
    return pl.pallas_call(
        restore_kernel,
        in_specs=[pl.BlockSpec(memory_space=pltpu.SMEM)] + [hbm] * 4,
        out_specs=hbm,
        out_shape=jax.ShapeDtypeStruct(shape, BF),
        scratch_shapes=[
            pltpu.VMEM(shape, BF),
            pltpu.SemaphoreType.DMA((16,)),
            pltpu.SemaphoreType.DMA,
        ],
        compiler_params=PARAMS,
        cost_estimate=COST,
        name="restore",
    )(places, *(block.reshape(4, 4, PIECE, WIDE) for block in blocks)).reshape(4096, WIDE)


def together(*values):
    return lax.optimization_barrier(values)


def state_kernel(cols_ref, key_ref, left_ref, right_ref, out_ref):
    for head, value_ref in enumerate((left_ref, right_ref)):
        weight = cols_ref[0, :, 4 + head : 5 + head]
        keys = key_ref[:, head * DQK : (head + 1) * DQK]
        scaled = (keys.astype(F32) * weight).astype(BF)
        out_ref[0, head] = lax.dot_general(
            scaled, value_ref[...], (((0,), (0,)), ((), ())), preferred_element_type=F32
        ).astype(BF)


def states(cols, held):
    parts = [pl.BlockSpec((ROWS, WIDE), lambda s, n=n: (s, n)) for n in range(3)]
    return pl.pallas_call(
        state_kernel,
        grid=(2,),
        in_specs=[pl.BlockSpec((1, ROWS, 8), lambda s: (s, 0, 0)), *parts],
        out_specs=pl.BlockSpec((1, 2, DQK, DV), lambda s: (s, 0, 0, 0)),
        out_shape=jax.ShapeDtypeStruct((2, 2, DQK, DV), BF),
        compiler_params=SMALL,
        cost_estimate=COST,
        name="states",
    )(cols, held, held, held)


def intra_kernel(cols_ref, rows_ref, query_ref, key_ref, left_ref, right_ref, out_ref):
    segment = cols_ref[0, :, 6:7]
    segment_row = rows_ref[0, 4:5, :]
    for head, value_ref in enumerate((left_ref, right_ref)):
        cumul = cols_ref[0, :, head : head + 1]
        cumul_row = rows_ref[0, head : head + 1, :]
        gate_row = rows_ref[0, 2 + head : 3 + head, :]
        features = slice(head * DQK, (head + 1) * DQK)
        for start, size in ((0, 256), (256, 384)):
            reach = start + size
            scores = lax.dot_general(
                query_ref[start:reach, features],
                key_ref[:reach, features],
                (((1,), (1,)), ((), ())),
                preferred_element_type=F32,
            ) * (DQK**-0.5)
            later = start + lax.broadcasted_iota(jnp.int32, (size, reach), 0)
            earlier = lax.broadcasted_iota(jnp.int32, (size, reach), 1)
            keep = (later >= earlier) & (segment[start:reach] == segment_row[:, :reach])
            diff = cumul[start:reach] - cumul_row[:, :reach] + gate_row[:, :reach]
            mixed = (scores * jnp.exp(jnp.where(keep, diff, -1e30))).astype(BF)
            out_ref[start:reach, head * DV : (head + 1) * DV] = jnp.dot(
                mixed, value_ref[:reach, :], preferred_element_type=F32
            )


def intra(cols, rows, query, held):
    parts = [pl.BlockSpec((ROWS, WIDE), lambda s, n=n: (s, n)) for n in (0, 0, 1, 2)]
    return pl.pallas_call(
        intra_kernel,
        grid=(2,),
        in_specs=[
            pl.BlockSpec((1, ROWS, 8), lambda s: (s, 0, 0)),
            pl.BlockSpec((1, 8, ROWS), lambda s: (s, 0, 0)),
            *parts,
        ],
        out_specs=pl.BlockSpec((ROWS, 2 * DV), lambda s: (s, 0)),
        out_shape=jax.ShapeDtypeStruct((2 * ROWS, 2 * DV), F32),
        compiler_params=SMALL,
        cost_estimate=COST,
        name="intra",
    )(cols, rows, query, held, held, held)


def readout_kernel(cols_ref, query_ref, intra_ref, carried_ref, out_ref):
    head = pl.program_id(0)
    reach = jnp.where(head == 0, cols_ref[0, :, 2:3], cols_ref[0, :, 3:4])
    between = jnp.dot(query_ref[...], carried_ref[0], preferred_element_type=F32) * reach
    readout = intra_ref[...] + between
    scale = lax.rsqrt(jnp.mean(readout * readout, axis=-1, keepdims=True) + 1e-05)
    out_ref[...] = (readout * scale).astype(BF)


def readout(slot, cols, qkv, inner, carried):
    return pl.pallas_call(
        readout_kernel,
        grid=(2,),
        in_specs=[
            pl.BlockSpec((1, ROWS, 8), lambda h: (slot, 0, 0)),
            pl.BlockSpec((ROWS, DQK), lambda h: (slot, h)),
            pl.BlockSpec((ROWS, DV), lambda h: (slot, h)),
            pl.BlockSpec((1, DQK, DV), lambda h: (h, 0, 0)),
        ],
        out_specs=pl.BlockSpec((ROWS, DV), lambda h: (0, h)),
        out_shape=jax.ShapeDtypeStruct((ROWS, 2 * DV), BF),
        compiler_params=SMALL,
        cost_estimate=COST,
        name="readout",
    )(cols, qkv, inner, carried)


def join(decay, earlier, later):
    return (decay.astype(F32)[:, None, None] * earlier.astype(F32) + later.astype(F32)).astype(BF)


def times(left, right):
    return (left.astype(F32) * right.astype(F32)).astype(BF)


def pack(state, decay):
    tail = jnp.broadcast_to(decay[:, None, None], (2, 8, DV))
    return jnp.concatenate([state, tail], axis=1)


def unpack(message):
    return message[:, :-8], message[:, -1, 0]


def in_order(mine, axis, send):
    place = lax.axis_index(axis)
    blocks = [mine] + [shift(send(by), axis, by) for by in (1, 2, 3)]
    stacked = jnp.stack(blocks)
    return [lax.dynamic_index_in_dim(stacked, (place - j) % 4, 0, False) for j in range(4)]


def carry_in(decay, state, query, more):
    x, z = lax.axis_index("x"), lax.axis_index("z")
    quarters = state.reshape(2, 4, DQK // 4, DV)

    def piece(by):
        return pack(lax.dynamic_index_in_dim(quarters, (x + by) % 4, 1, False), decay)

    line = [unpack(block) for block in in_order(piece(0), "x", piece)]
    prior = jnp.zeros_like(line[0][0])
    reach = jnp.ones_like(decay)
    priors, reaches = [], []
    for block, fade in line:
        priors.append(prior)
        reaches.append(reach)
        prior = join(fade, prior, block)
        reach = times(fade, reach)
    whole, query = together(pack(prior, reach), query)
    before = jnp.zeros_like(prior)
    for j, message in enumerate(in_order(whole, "z", lambda by: whole)):
        block, fade = unpack(message)
        before = jnp.where(j < z, join(fade, before, block), before)
    backs = jnp.stack([join(reaches[j], before, priors[j]) for j in range(4)])
    backs, inner = together(backs, more(query))

    def back(by):
        return lax.dynamic_index_in_dim(backs, (x + by) % 4, 0, False)

    return jnp.stack(in_order(back(0), "x", back), axis=1).reshape(2, DQK, DV), inner


def gate_rows(w_gates, core, place):
    gates = w_gates.T.reshape(2, 2, 2, OWN).transpose(1, 0, 2, 3).reshape(2, 4, OWN)
    mate = swap(gates)
    gates = jnp.where(
        core == 0,
        jnp.concatenate([gates[0], mate[0]], axis=1),
        jnp.concatenate([mate[1], gates[1]], axis=1),
    )
    gates = jnp.pad(gates.reshape(1, 4 * PIECE), ((0, 0), (0, WIDE - 4 * PIECE)))
    row = lax.broadcasted_iota(jnp.int32, (EXTRA, WIDE), 0)
    return jnp.where(row == place, gates, jnp.zeros_like(gates))


def per_device(tokens, w_query, w_key, w_value, w_gates, forget_bias, doc_lengths):
    core = lax.axis_index("core")
    y, z, x = lax.axis_index("y"), lax.axis_index("z"), lax.axis_index("x")
    chip = z * 4 + x
    last, middle = jnp.where(core == 0, x, z), jnp.where(core == 0, z, x)
    core_scalar = core[None].astype(jnp.int32)
    restore_places = jnp.concatenate([places(last), core_scalar])

    own = (w_query, w_key, w_value)
    mate = tuple(swap(weight) for weight in own)
    held, rest = prepare(core_scalar, own, mate, gate_rows(w_gates, core, middle * 4 + y))
    rest = lax.all_gather(rest, ("y", "z", "x"), axis=0, tiled=True)
    tokens = together(tokens[0], held)[0]
    normed = normalize(tokens, swap(tokens))

    (held,) = assemble(places(y), together(*around(held, "yy")), PIECE, False)
    held, region = assemble(places(middle), together(*around(held, "zx")), 4 * PIECE, True)
    regions = jnp.stack(together(*around(region, "xz")))
    regions = jnp.stack([lax.dynamic_index_in_dim(regions, (j - last) % 4, 0, False) for j in range(4)])
    regions = regions[:, :, : 4 * PIECE].reshape(4, 4, 4, 4, PIECE)
    w_gates = jnp.where(
        core == 0, regions.transpose(3, 2, 1, 0, 4), regions.transpose(3, 2, 0, 1, 4)
    ).reshape(4, 4096)
    gates = lax.dot_general(
        normed, w_gates, (((1,), (1,)), ((), ())), preferred_element_type=F32
    )
    held, rest, gates = together(held, rest, gates)
    blocks = around(held, "xz")

    gates = gates.reshape(2, ROWS, 4)
    lengths = doc_lengths[0]
    starts = jnp.cumsum(lengths) - lengths
    shard = chip * 2 + jnp.stack([core, 1 - core])
    positions = shard[:, None] * ROWS + jnp.arange(ROWS, dtype=jnp.int32)[None, :]
    resets = jnp.any(positions[:, :, None] == starts[None, None, :], axis=-1)
    bias = lax.dynamic_slice_in_dim(forget_bias, core * 2, 2)
    in_gate = gates[:, :, :2]
    cumul = jnp.cumsum(jax.nn.log_sigmoid(gates[:, :, 2:] + bias), axis=1)
    segment = jnp.cumsum(resets.astype(jnp.int32), axis=1)
    last = cumul[:, -1]
    same = (segment == segment[:, -1:])[:, :, None]
    weight = jnp.exp(jnp.where(same, last[:, None, :] - cumul + in_gate, -1e30))
    decay = (jnp.exp(last) * (segment[:, -1:] == 0).astype(F32)).astype(BF)
    reach = jnp.exp(cumul) * (segment == 0).astype(F32)[:, :, None] * (DQK**-0.5)
    seg = segment.astype(F32)[:, :, None]
    cols = jnp.concatenate([cumul, reach, weight, seg, jnp.zeros_like(seg)], axis=2)
    rows = jnp.concatenate([cumul, in_gate, seg, jnp.zeros_like(seg), weight], axis=2)
    rows = rows.transpose(0, 2, 1)

    rest, cols, rows, decay, restore_places = together(rest, cols, rows, decay, restore_places)
    held = jnp.dot(normed, rest, preferred_element_type=F32).astype(BF)
    state = states(cols, held)
    *blocks, state = together(*blocks, state)
    w_query = restore(restore_places, blocks)
    query = jnp.dot(normed, w_query, preferred_element_type=F32).astype(BF)
    first = lax.dynamic_index_in_dim(state, core, 0, False)
    second = lax.dynamic_index_in_dim(state, 1 - core, 0, False)
    fade_first = lax.dynamic_index_in_dim(decay, core, 0, False)
    fade_second = lax.dynamic_index_in_dim(decay, 1 - core, 0, False)
    chip_state = join(fade_second, first, second)
    carried, inner = carry_in(
        times(fade_first, fade_second), chip_state, query, lambda query: intra(cols, rows, query, held)
    )
    carried_second = join(fade_first, carried, first)
    mine = jnp.where(core == 0, carried, carried_second)
    other = jnp.where(core == 0, carried_second, carried)
    outgoing = readout(1, cols, query, inner, other)
    incoming = swap(outgoing)
    kept = readout(0, cols, query, inner, mine)
    result = jnp.where(
        core == 0,
        jnp.concatenate([kept, incoming], axis=1),
        jnp.concatenate([incoming, kept], axis=1),
    )
    return result.reshape(1, ROWS, 2048)


def solution(mesh):
    split = Mesh(mesh.devices.reshape(4, 4, 4, 2), ("y", "z", "x", "core"))
    weight_spec = P(("y", "z", "x", "core"), None)
    in_specs = (
        P("y", ("z", "x", "core"), None),
        weight_spec,
        weight_spec,
        weight_spec,
        weight_spec,
        P(),
        P("y", None),
    )
    out_specs = P("y", ("z", "x", "core"), None)
    return jax.shard_map(
        per_device, mesh=split, in_specs=in_specs, out_specs=out_specs, check_vma=False
    )
```

```python
import functools
import itertools

import jax
import jax.numpy as jnp
from jax import lax
from jax.experimental import pallas as pl
from jax.experimental.pallas import tpu as pltpu
from jax.sharding import Mesh, PartitionSpec as P

ROWS = 640
DQK = 256
DV = 512
OWN = 32
PIECE = 64
EXTRA = 16
WIDE = 512
BF = jnp.bfloat16
F32 = jnp.float32
COST = pl.CostEstimate(flops=0, bytes_accessed=1 << 10, transcendentals=0)
SMALL = pltpu.CompilerParams(vmem_limit_bytes=20 * 1024 * 1024)
PARAMS = pltpu.CompilerParams(vmem_limit_bytes=20 * 1024 * 1024)


def swap(value):
    return lax.ppermute(value, "core", [(0, 1), (1, 0)])


def shift(value, axis, by):
    return lax.ppermute(value, axis, [(i, (i + by) % 4) for i in range(4)])


def hop(value, axes, by):
    names, pairs = ("y", "z", "x", "core"), []
    for source in itertools.product(range(4), range(4), range(4), range(2)):
        target = list(source)
        at = names.index(axes[source[3]])
        target[at] = (target[at] + by) % 4
        flat = [((p[0] * 4 + p[1]) * 4 + p[2]) * 2 + p[3] for p in (source, target)]
        pairs.append(tuple(flat))
    return lax.ppermute(value, names, pairs)


def around(value, axes):
    return (value,) + tuple(hop(value, axes, by) for by in (3, 2, 1))


def places(at):
    return jnp.stack([at, (at + 1) % 4, (at + 2) % 4, (at + 3) % 4]).astype(jnp.int32)


def normalize_kernel(places, own_ref, mate_ref, out_ref, *refs):
    chunks, scratch = refs[:4], refs[4]
    raw = jnp.where(pl.program_id(0) == 0, own_ref[...], mate_ref[...])
    values = raw.astype(F32)
    scale = lax.rsqrt(jnp.mean(values * values, axis=-1, keepdims=True) + 1e-06)
    normed = (values * scale).astype(BF)
    out_ref[...] = normed

    def reorder(last_step, other_step):
        for last in range(4):
            for other in range(4):
                for pair in range(2):
                    halves = []
                    for y in (2 * pair, 2 * pair + 1):
                        start = y * 1024 + last * last_step + other * other_step
                        halves.append(out_ref[:, start : start + 64])
                    start = last * 1024 + other * 256 + pair * 128
                    scratch[:, start : start + 128] = jnp.concatenate(halves, axis=1)

    pl.when(places[4] == 0)(lambda: reorder(64, 256))
    pl.when(places[4] == 1)(lambda: reorder(256, 64))
    for which in range(4):
        start = pl.multiple_of(places[which] * 1024, 1024)
        chunks[which][...] = scratch[:, pl.ds(start, 1024)]


def normalize(places, own, mate):
    tile = 128
    steps = ROWS // tile
    return pl.pallas_call(
        normalize_kernel,
        grid_spec=pltpu.PrefetchScalarGridSpec(
            num_scalar_prefetch=1,
            grid=(2, steps),
            in_specs=[
                pl.BlockSpec((tile, 4096), lambda s, i, p: (jnp.where(s == 0, i, steps - 1), 0)),
                pl.BlockSpec((tile, 4096), lambda s, i, p: (jnp.where(s == 0, 0, i), 0)),
            ],
            out_specs=[pl.BlockSpec((tile, 4096), lambda s, i, p: (s * steps + i, 0))]
            + [pl.BlockSpec((tile, 1024), lambda s, i, p: (s * steps + i, 0))] * 4,
            scratch_shapes=[pltpu.VMEM((tile, 4096), BF)],
        ),
        out_shape=[jax.ShapeDtypeStruct((2 * ROWS, 4096), BF)]
        + [jax.ShapeDtypeStruct((2 * ROWS, 1024), BF)] * 4,
        compiler_params=PARAMS,
        cost_estimate=pl.CostEstimate(flops=0, bytes_accessed=32 << 20, transcendentals=0),
        name="normalize",
    )(places, own, mate)


def prepare_kernel(core_ref, query, key, mate_query, mate_key, region, held_ref, q_ref):
    core = core_ref[0]
    narrow = pl.ds(pl.multiple_of(core * WIDE, WIDE), WIDE)
    for queries, keys, rows in ((query, key, core), (mate_query, mate_key, 1 - core)):
        rows = pl.ds(pl.multiple_of(rows * OWN, OWN), OWN)
        q_ref[rows, :] = queries[:, narrow]
        held_ref[rows, :] = keys[:, narrow]
    held_ref[PIECE:, :] = region[...]


def prepare(core, own, mate, region):
    vmem = pl.BlockSpec(memory_space=pltpu.VMEM)
    return pl.pallas_call(
        prepare_kernel,
        in_specs=[pl.BlockSpec(memory_space=pltpu.SMEM)] + [vmem] * 5,
        out_specs=[vmem] * 2,
        out_shape=[
            jax.ShapeDtypeStruct((PIECE + EXTRA, WIDE), BF),
            jax.ShapeDtypeStruct((PIECE, WIDE), BF),
        ],
        compiler_params=PARAMS,
        cost_estimate=COST,
        name="prepare",
    )(core, *own, *mate, region)


def weave_kernel(groups, places, *refs):
    blocks, out, held, sems_in, sem_out = refs[:4], *refs[4:]

    def run(target):
        copies = [
            pltpu.make_async_copy(block, target(places[which]), sems_in.at[which])
            for which, block in enumerate(blocks)
        ]
        for copy in copies:
            copy.start()
        for copy in copies:
            copy.wait()

    if groups:
        pl.when(places[4] == 0)(lambda: run(lambda place: held.at[:, place]))
        pl.when(places[4] == 1)(lambda: run(lambda place: held.at[place]))
    else:
        run(lambda place: held.at[place])
    store = pltpu.make_async_copy(held, out, sem_out)
    store.start()
    store.wait()


def weave(places, blocks, groups):
    hbm = pl.BlockSpec(memory_space=pl.ANY)
    shape = (4, 4, PIECE, WIDE) if groups else (4, PIECE, WIDE)
    blocks = [block.reshape(shape[1:]) for block in blocks]
    return pl.pallas_call(
        functools.partial(weave_kernel, groups),
        in_specs=[pl.BlockSpec(memory_space=pltpu.SMEM)] + [hbm] * 4,
        out_specs=hbm,
        out_shape=jax.ShapeDtypeStruct(shape, BF),
        scratch_shapes=[
            pltpu.VMEM(shape, BF),
            pltpu.SemaphoreType.DMA((4,)),
            pltpu.SemaphoreType.DMA,
        ],
        compiler_params=PARAMS,
        cost_estimate=COST,
        name="weave",
    )(places, *blocks).reshape(-1, WIDE)


def assemble_kernel(rows, final, places, *refs):
    blocks, out, held, regions, sems_in, sems_more, sems_out = refs[:4], refs[4:-5], *refs[-5:]
    loads, extras = [], []
    for which, block in enumerate(blocks):
        start = pl.multiple_of(places[which] * rows, PIECE)
        loads.append(
            pltpu.make_async_copy(
                block.at[pl.ds(0, rows), :], held.at[pl.ds(start, rows), :], sems_in.at[which]
            )
        )
        extras.append(
            pltpu.make_async_copy(
                block.at[pl.ds(rows, EXTRA), :], regions.at[which], sems_more.at[which]
            )
        )
    for copy in extras + loads:
        copy.start()
    for copy in extras:
        copy.wait()
    held[4 * rows :, :] = (regions[0] + regions[1]) + (regions[2] + regions[3])
    for copy in loads:
        copy.wait()
    if final:
        stores = [
            pltpu.make_async_copy(held.at[pl.ds(0, 4 * rows), :], out[0], sems_out.at[0]),
            pltpu.make_async_copy(held.at[pl.ds(4 * rows, EXTRA), :], out[1], sems_out.at[1]),
        ]
    else:
        stores = [pltpu.make_async_copy(held, out[0], sems_out.at[0])]
    for copy in stores:
        copy.start()
    for copy in stores:
        copy.wait()


def assemble(places, blocks, rows, final):
    hbm = pl.BlockSpec(memory_space=pl.ANY)
    if final:
        shapes = [(4 * rows, WIDE), (EXTRA, WIDE)]
    else:
        shapes = [(4 * rows + EXTRA, WIDE)]
    return pl.pallas_call(
        functools.partial(assemble_kernel, rows, final),
        in_specs=[pl.BlockSpec(memory_space=pltpu.SMEM)] + [hbm] * 4,
        out_specs=[hbm] * len(shapes),
        out_shape=[jax.ShapeDtypeStruct(shape, BF) for shape in shapes],
        scratch_shapes=[
            pltpu.VMEM((4 * rows + EXTRA, WIDE), BF),
            pltpu.VMEM((4, EXTRA, WIDE), BF),
            pltpu.SemaphoreType.DMA((4,)),
            pltpu.SemaphoreType.DMA((4,)),
            pltpu.SemaphoreType.DMA((2,)),
        ],
        compiler_params=PARAMS,
        cost_estimate=COST,
        name="assemble",
    )(places, *blocks)


def together(*values):
    return lax.optimization_barrier(values)


def project(chunks, weights, total=None):
    for chunk, weight in zip(chunks, weights):
        term = jnp.dot(chunk, weight, preferred_element_type=F32)
        total = term if total is None else total + term
    return total


def state_kernel(cols_ref, key_ref, left_ref, right_ref, out_ref):
    for head, value_ref in enumerate((left_ref, right_ref)):
        weight = cols_ref[0, :, 4 + head : 5 + head]
        keys = key_ref[:, head * DQK : (head + 1) * DQK]
        scaled = (keys.astype(F32) * weight).astype(BF)
        out_ref[0, head] = lax.dot_general(
            scaled, value_ref[...], (((0,), (0,)), ((), ())), preferred_element_type=F32
        ).astype(BF)


def states(cols, key, value):
    parts = [pl.BlockSpec((ROWS, WIDE), lambda s, n=n: (s, n)) for n in (0, 0, 1)]
    return pl.pallas_call(
        state_kernel,
        grid=(2,),
        in_specs=[pl.BlockSpec((1, ROWS, 8), lambda s: (s, 0, 0)), *parts],
        out_specs=pl.BlockSpec((1, 2, DQK, DV), lambda s: (s, 0, 0, 0)),
        out_shape=jax.ShapeDtypeStruct((2, 2, DQK, DV), BF),
        compiler_params=SMALL,
        cost_estimate=COST,
        name="states",
    )(cols, key, value, value)


def intra_kernel(cols_ref, rows_ref, query_ref, key_ref, left_ref, right_ref, out_ref):
    segment = cols_ref[0, :, 6:7]
    segment_row = rows_ref[0, 4:5, :]
    for head, value_ref in enumerate((left_ref, right_ref)):
        cumul = cols_ref[0, :, head : head + 1]
        cumul_row = rows_ref[0, head : head + 1, :]
        gate_row = rows_ref[0, 2 + head : 3 + head, :]
        features = slice(head * DQK, (head + 1) * DQK)
        for start, size in ((0, 256), (256, 384)):
            reach = start + size
            scores = lax.dot_general(
                query_ref[start:reach, features],
                key_ref[:reach, features],
                (((1,), (1,)), ((), ())),
                preferred_element_type=F32,
            ) * (DQK**-0.5)
            later = start + lax.broadcasted_iota(jnp.int32, (size, reach), 0)
            earlier = lax.broadcasted_iota(jnp.int32, (size, reach), 1)
            keep = (later >= earlier) & (segment[start:reach] == segment_row[:, :reach])
            diff = cumul[start:reach] - cumul_row[:, :reach] + gate_row[:, :reach]
            mixed = (scores * jnp.exp(jnp.where(keep, diff, -1e30))).astype(BF)
            out_ref[start:reach, head * DV : (head + 1) * DV] = jnp.dot(
                mixed, value_ref[:reach, :], preferred_element_type=F32
            )


def intra(cols, rows, query, key, value):
    parts = [pl.BlockSpec((ROWS, WIDE), lambda s, n=n: (s, n)) for n in (0, 0, 0, 1)]
    return pl.pallas_call(
        intra_kernel,
        grid=(2,),
        in_specs=[
            pl.BlockSpec((1, ROWS, 8), lambda s: (s, 0, 0)),
            pl.BlockSpec((1, 8, ROWS), lambda s: (s, 0, 0)),
            *parts,
        ],
        out_specs=pl.BlockSpec((ROWS, 2 * DV), lambda s: (s, 0)),
        out_shape=jax.ShapeDtypeStruct((2 * ROWS, 2 * DV), F32),
        compiler_params=SMALL,
        cost_estimate=COST,
        name="intra",
    )(cols, rows, query, key, value, value)


def readout_kernel(cols_ref, query_ref, intra_ref, carried_ref, out_ref):
    head = pl.program_id(0)
    reach = jnp.where(head == 0, cols_ref[0, :, 2:3], cols_ref[0, :, 3:4])
    between = jnp.dot(query_ref[...], carried_ref[0], preferred_element_type=F32) * reach
    readout = intra_ref[...] + between
    scale = lax.rsqrt(jnp.mean(readout * readout, axis=-1, keepdims=True) + 1e-05)
    out_ref[...] = (readout * scale).astype(BF)


def readout(slot, cols, qkv, inner, carried):
    return pl.pallas_call(
        readout_kernel,
        grid=(2,),
        in_specs=[
            pl.BlockSpec((1, ROWS, 8), lambda h: (slot, 0, 0)),
            pl.BlockSpec((ROWS, DQK), lambda h: (slot, h)),
            pl.BlockSpec((ROWS, DV), lambda h: (slot, h)),
            pl.BlockSpec((1, DQK, DV), lambda h: (h, 0, 0)),
        ],
        out_specs=pl.BlockSpec((ROWS, DV), lambda h: (0, h)),
        out_shape=jax.ShapeDtypeStruct((ROWS, 2 * DV), BF),
        compiler_params=SMALL,
        cost_estimate=COST,
        name="readout",
    )(cols, qkv, inner, carried)


def join(decay, earlier, later):
    return (decay.astype(F32)[:, None, None] * earlier.astype(F32) + later.astype(F32)).astype(BF)


def times(left, right):
    return (left.astype(F32) * right.astype(F32)).astype(BF)


def pack(state, decay):
    tail = jnp.broadcast_to(decay[:, None, None], (2, 8, DV))
    return jnp.concatenate([state, tail], axis=1)


def unpack(message):
    return message[:, :-8], message[:, -1, 0]


def in_order(mine, axis, send):
    place = lax.axis_index(axis)
    blocks = [mine] + [shift(send(by), axis, by) for by in (1, 2, 3)]
    stacked = jnp.stack(blocks)
    return [lax.dynamic_index_in_dim(stacked, (place - j) % 4, 0, False) for j in range(4)]


def carry_in(decay, state, beside):
    x, z = lax.axis_index("x"), lax.axis_index("z")
    quarters = state.reshape(2, 4, DQK // 4, DV)

    def piece(by):
        return pack(lax.dynamic_index_in_dim(quarters, (x + by) % 4, 1, False), decay)

    line = [unpack(block) for block in in_order(piece(0), "x", piece)]
    prior = jnp.zeros_like(line[0][0])
    reach = jnp.ones_like(decay)
    priors, reaches = [], []
    for block, fade in line:
        priors.append(prior)
        reaches.append(reach)
        prior = join(fade, prior, block)
        reach = times(fade, reach)
    whole, done = together(pack(prior, reach), beside[0]())
    before = jnp.zeros_like(prior)
    for j, message in enumerate(in_order(whole, "z", lambda by: whole)):
        block, fade = unpack(message)
        before = jnp.where(j < z, join(fade, before, block), before)
    backs = jnp.stack([join(reaches[j], before, priors[j]) for j in range(4)])
    backs, done = together(backs, beside[1](done))

    def back(by):
        return lax.dynamic_index_in_dim(backs, (x + by) % 4, 0, False)

    inner = beside[2](done)
    carried, inner = together(jnp.stack(in_order(back(0), "x", back), axis=1), inner)
    return carried.reshape(2, DQK, DV), done, inner


def gate_rows(w_gates, core, place):
    gates = w_gates.T.reshape(2, 2, 2, OWN).transpose(1, 0, 2, 3).reshape(2, 4, OWN)
    mate = swap(gates)
    gates = jnp.where(
        core == 0,
        jnp.concatenate([gates[0], mate[0]], axis=1),
        jnp.concatenate([mate[1], gates[1]], axis=1),
    )
    gates = jnp.pad(gates.reshape(1, 4 * PIECE), ((0, 0), (0, WIDE - 4 * PIECE)))
    row = lax.broadcasted_iota(jnp.int32, (EXTRA, WIDE), 0)
    return jnp.where(row == place, gates, jnp.zeros_like(gates))


def per_device(tokens, w_query, w_key, w_value, w_gates, forget_bias, doc_lengths):
    core = lax.axis_index("core")
    y, z, x = lax.axis_index("y"), lax.axis_index("z"), lax.axis_index("x")
    chip = z * 4 + x
    last, middle = jnp.where(core == 0, x, z), jnp.where(core == 0, z, x)
    core_scalar = core[None].astype(jnp.int32)
    restore_places = jnp.concatenate([places(last), core_scalar])
    q_places = jnp.concatenate([places(middle), core_scalar])

    rest = lax.all_gather(w_value, ("y", "z", "x", "core"), axis=0, tiled=True)
    own = (w_query, w_key)
    mate = tuple(swap(weight) for weight in own)
    held, columns = prepare(core_scalar, own, mate, gate_rows(w_gates, core, middle * 4 + y))
    tokens = together(tokens[0], held)[0]
    normed, *chunks = normalize(restore_places, tokens, swap(tokens))

    (held,) = assemble(places(y), together(*around(held, "yy")), PIECE, False)
    held, columns = together(held, columns)
    columns = weave(q_places, together(*around(columns, "zx")), False)
    held, region = assemble(places(middle), together(*around(held, "zx")), 4 * PIECE, True)
    columns = weave(restore_places, together(*around(columns, "xz")), True)
    regions = jnp.stack(together(*around(region, "xz")))
    regions = jnp.stack([lax.dynamic_index_in_dim(regions, (j - last) % 4, 0, False) for j in range(4)])
    regions = regions[:, :, : 4 * PIECE].reshape(4, 4, 4, 4, PIECE)
    w_gates = jnp.where(
        core == 0, regions.transpose(3, 2, 1, 0, 4), regions.transpose(3, 2, 0, 1, 4)
    ).reshape(4, 4096)
    gates = lax.dot_general(
        normed, w_gates, (((1,), (1,)), ((), ())), preferred_element_type=F32
    )
    key = project(chunks[:1], [held])
    held, columns, rest, gates, key = together(held, columns, rest, gates, key)
    blocks = around(held, "xz")
    columns = around(columns, "yy")

    gates = gates.reshape(2, ROWS, 4)
    lengths = doc_lengths[0]
    starts = jnp.cumsum(lengths) - lengths
    shard = chip * 2 + jnp.stack([core, 1 - core])
    positions = shard[:, None] * ROWS + jnp.arange(ROWS, dtype=jnp.int32)[None, :]
    resets = jnp.any(positions[:, :, None] == starts[None, None, :], axis=-1)
    bias = lax.dynamic_slice_in_dim(forget_bias, core * 2, 2)
    in_gate = gates[:, :, :2]
    cumul = jnp.cumsum(jax.nn.log_sigmoid(gates[:, :, 2:] + bias), axis=1)
    segment = jnp.cumsum(resets.astype(jnp.int32), axis=1)
    last = cumul[:, -1]
    same = (segment == segment[:, -1:])[:, :, None]
    weight = jnp.exp(jnp.where(same, last[:, None, :] - cumul + in_gate, -1e30))
    decay = (jnp.exp(last) * (segment[:, -1:] == 0).astype(F32)).astype(BF)
    reach = jnp.exp(cumul) * (segment == 0).astype(F32)[:, :, None] * (DQK**-0.5)
    seg = segment.astype(F32)[:, :, None]
    cols = jnp.concatenate([cumul, reach, weight, seg, jnp.zeros_like(seg)], axis=2)
    rows = jnp.concatenate([cumul, in_gate, seg, jnp.zeros_like(seg), weight], axis=2)
    rows = rows.transpose(0, 2, 1)

    rest, cols, rows, decay = together(rest, cols, rows, decay)
    value = lax.cond(
        core == 0,
        lambda normed, rest: jnp.dot(normed, rest[:, : 2 * WIDE], preferred_element_type=F32).astype(BF),
        lambda normed, rest: jnp.dot(normed, rest[:, 2 * WIDE :], preferred_element_type=F32).astype(BF),
        normed,
        rest,
    )
    key = project(chunks[1:], blocks[1:], key).astype(BF)
    state = states(cols, key, value)
    first = lax.dynamic_index_in_dim(state, core, 0, False)
    second = lax.dynamic_index_in_dim(state, 1 - core, 0, False)
    fade_first = lax.dynamic_index_in_dim(decay, core, 0, False)
    fade_second = lax.dynamic_index_in_dim(decay, 1 - core, 0, False)
    chip_state = join(fade_second, first, second)
    by_y = [lax.dynamic_slice_in_dim(normed, ((y + n) % 4) * 1024, 1024, 1) for n in range(4)]
    carried, query, inner = carry_in(
        times(fade_first, fade_second),
        chip_state,
        (
            lambda: project(by_y[:2], columns[:2]),
            lambda total: project(by_y[2:], columns[2:], total).astype(BF),
            lambda query: intra(cols, rows, query, key, value),
        ),
    )
    carried_second = join(fade_first, carried, first)
    mine = jnp.where(core == 0, carried, carried_second)
    other = jnp.where(core == 0, carried_second, carried)
    outgoing = readout(1, cols, query, inner, other)
    incoming = swap(outgoing)
    kept = readout(0, cols, query, inner, mine)
    result = jnp.where(
        core == 0,
        jnp.concatenate([kept, incoming], axis=1),
        jnp.concatenate([incoming, kept], axis=1),
    )
    return result.reshape(1, ROWS, 2048)


def solution(mesh):
    split = Mesh(mesh.devices.reshape(4, 4, 4, 2), ("y", "z", "x", "core"))
    weight_spec = P(("y", "z", "x", "core"), None)
    in_specs = (
        P("y", ("z", "x", "core"), None),
        weight_spec,
        weight_spec,
        weight_spec,
        weight_spec,
        P(),
        P("y", None),
    )
    out_specs = P("y", ("z", "x", "core"), None)
    return jax.shard_map(
        per_device, mesh=split, in_specs=in_specs, out_specs=out_specs, check_vma=False
    )
```

```python
import functools
import itertools

import jax
import jax.numpy as jnp
from jax import lax
from jax.experimental import pallas as pl
from jax.experimental.pallas import tpu as pltpu
from jax.sharding import Mesh, PartitionSpec as P

ROWS = 640
DQK = 256
DV = 512
OWN = 32
PIECE = 64
EXTRA = 16
WIDE = 512
BF = jnp.bfloat16
F32 = jnp.float32
COST = pl.CostEstimate(flops=0, bytes_accessed=1 << 10, transcendentals=0)
SMALL = pltpu.CompilerParams(vmem_limit_bytes=20 * 1024 * 1024)
PARAMS = pltpu.CompilerParams(vmem_limit_bytes=20 * 1024 * 1024)


def swap(value):
    return lax.ppermute(value, "core", [(0, 1), (1, 0)])


def shift(value, axis, by):
    return lax.ppermute(value, axis, [(i, (i + by) % 4) for i in range(4)])


def hop(value, axes, by):
    names, pairs = ("y", "z", "x", "core"), []
    for source in itertools.product(range(4), range(4), range(4), range(2)):
        target = list(source)
        at = names.index(axes[source[3]])
        target[at] = (target[at] + by) % 4
        flat = [((p[0] * 4 + p[1]) * 4 + p[2]) * 2 + p[3] for p in (source, target)]
        pairs.append(tuple(flat))
    return lax.ppermute(value, names, pairs)


def around(value, axes):
    return (value,) + tuple(hop(value, axes, by) for by in (3, 2, 1))


def places(at):
    return jnp.stack([at, (at + 1) % 4, (at + 2) % 4, (at + 3) % 4]).astype(jnp.int32)


def normalize_kernel(places, own_ref, mate_ref, w_gates_ref, gates_ref, out_ref, *refs):
    chunks, by_y, scratch = refs[:4], refs[4:8], refs[8]
    raw = jnp.where(pl.program_id(0) == 0, own_ref[...], mate_ref[...])
    values = raw.astype(F32)
    scale = lax.rsqrt(jnp.mean(values * values, axis=-1, keepdims=True) + 1e-06)
    normed = (values * scale).astype(BF)
    out_ref[...] = normed
    gates_ref[...] = lax.dot_general(
        w_gates_ref[...], normed, (((1,), (1,)), ((), ())), preferred_element_type=F32
    )

    def reorder(last_step, other_step):
        for last in range(4):
            for other in range(4):
                for pair in range(2):
                    halves = []
                    for y in (2 * pair, 2 * pair + 1):
                        start = y * 1024 + last * last_step + other * other_step
                        halves.append(out_ref[:, start : start + 64])
                    start = last * 1024 + other * 256 + pair * 128
                    scratch[:, start : start + 128] = jnp.concatenate(halves, axis=1)

    pl.when(places[4] == 0)(lambda: reorder(64, 256))
    pl.when(places[4] == 1)(lambda: reorder(256, 64))
    for which in range(4):
        start = pl.multiple_of(places[which] * 1024, 1024)
        chunks[which][...] = scratch[:, pl.ds(start, 1024)]
        start = pl.multiple_of(places[5 + which] * 1024, 1024)
        by_y[which][...] = out_ref[:, pl.ds(start, 1024)]


def normalize(places, own, mate, w_gates):
    tile = 128
    steps = ROWS // tile
    return pl.pallas_call(
        normalize_kernel,
        grid_spec=pltpu.PrefetchScalarGridSpec(
            num_scalar_prefetch=1,
            grid=(2, steps),
            in_specs=[
                pl.BlockSpec((tile, 4096), lambda s, i, p: (jnp.where(s == 0, i, steps - 1), 0)),
                pl.BlockSpec((tile, 4096), lambda s, i, p: (jnp.where(s == 0, 0, i), 0)),
                pl.BlockSpec((EXTRA, 4096), lambda s, i, p: (0, 0)),
            ],
            out_specs=[pl.BlockSpec((EXTRA, tile), lambda s, i, p: (0, s * steps + i))]
            + [pl.BlockSpec((tile, 4096), lambda s, i, p: (s * steps + i, 0))]
            + [pl.BlockSpec((tile, 1024), lambda s, i, p: (s * steps + i, 0))] * 8,
            scratch_shapes=[pltpu.VMEM((tile, 4096), BF)],
        ),
        out_shape=[
            jax.ShapeDtypeStruct((EXTRA, 2 * ROWS), F32),
            jax.ShapeDtypeStruct((2 * ROWS, 4096), BF),
        ]
        + [jax.ShapeDtypeStruct((2 * ROWS, 1024), BF)] * 8,
        compiler_params=PARAMS,
        cost_estimate=pl.CostEstimate(flops=0, bytes_accessed=32 << 20, transcendentals=0),
        name="normalize",
    )(places, own, mate, w_gates)


def prepare_kernel(
    core_ref, query, key, value, mate_query, mate_key, mate_value, region, held_ref, q_ref, rest_ref
):
    core = core_ref[0]
    narrow = pl.ds(pl.multiple_of(core * WIDE, WIDE), WIDE)
    wide = pl.ds(pl.multiple_of(core * 2 * WIDE, WIDE), 2 * WIDE)
    for source, rows in (((query, key, value), core), ((mate_query, mate_key, mate_value), 1 - core)):
        rows = pl.ds(pl.multiple_of(rows * OWN, OWN), OWN)
        q_ref[rows, :] = source[0][:, narrow]
        held_ref[rows, :] = source[1][:, narrow]
        rest_ref[rows, :] = source[2][:, wide]
    held_ref[PIECE:, :] = region[...]


def prepare(core, own, mate, region):
    vmem = pl.BlockSpec(memory_space=pltpu.VMEM)
    return pl.pallas_call(
        prepare_kernel,
        in_specs=[pl.BlockSpec(memory_space=pltpu.SMEM)] + [vmem] * 7,
        out_specs=[vmem] * 3,
        out_shape=[
            jax.ShapeDtypeStruct((PIECE + EXTRA, WIDE), BF),
            jax.ShapeDtypeStruct((PIECE, WIDE), BF),
            jax.ShapeDtypeStruct((PIECE, 2 * WIDE), BF),
        ],
        compiler_params=PARAMS,
        cost_estimate=COST,
        name="prepare",
    )(core, *own, *mate, region)


def weave_kernel(groups, places, *refs):
    blocks, out, held, sems_in, sem_out = refs[:4], *refs[4:]

    def run(target):
        copies = [
            pltpu.make_async_copy(block, target(places[which]), sems_in.at[which])
            for which, block in enumerate(blocks)
        ]
        for copy in copies:
            copy.start()
        for copy in copies:
            copy.wait()

    if groups:
        pl.when(places[4] == 0)(lambda: run(lambda place: held.at[:, place]))
        pl.when(places[4] == 1)(lambda: run(lambda place: held.at[place]))
    else:
        run(lambda place: held.at[place])
    store = pltpu.make_async_copy(held, out, sem_out)
    store.start()
    store.wait()


def weave(places, blocks, groups):
    hbm = pl.BlockSpec(memory_space=pl.ANY)
    shape = (4, 4, PIECE, WIDE) if groups else (4, PIECE, WIDE)
    blocks = [block.reshape(shape[1:]) for block in blocks]
    return pl.pallas_call(
        functools.partial(weave_kernel, groups),
        in_specs=[pl.BlockSpec(memory_space=pltpu.SMEM)] + [hbm] * 4,
        out_specs=hbm,
        out_shape=jax.ShapeDtypeStruct(shape, BF),
        scratch_shapes=[
            pltpu.VMEM(shape, BF),
            pltpu.SemaphoreType.DMA((4,)),
            pltpu.SemaphoreType.DMA,
        ],
        compiler_params=PARAMS,
        cost_estimate=COST,
        name="weave",
    )(places, *blocks).reshape(-1, WIDE)


def assemble_kernel(rows, final, places, *refs):
    blocks, out, held, regions, sems_in, sems_more, sems_out = refs[:4], refs[4:-5], *refs[-5:]
    loads, extras = [], []
    for which, block in enumerate(blocks):
        start = pl.multiple_of(places[which] * rows, PIECE)
        loads.append(
            pltpu.make_async_copy(
                block.at[pl.ds(0, rows), :], held.at[pl.ds(start, rows), :], sems_in.at[which]
            )
        )
        extras.append(
            pltpu.make_async_copy(
                block.at[pl.ds(rows, EXTRA), :], regions.at[which], sems_more.at[which]
            )
        )
    for copy in extras + loads:
        copy.start()
    for copy in extras:
        copy.wait()
    held[4 * rows :, :] = (regions[0] + regions[1]) + (regions[2] + regions[3])
    for copy in loads:
        copy.wait()
    if final:
        stores = [
            pltpu.make_async_copy(held.at[pl.ds(0, 4 * rows), :], out[0], sems_out.at[0]),
            pltpu.make_async_copy(held.at[pl.ds(4 * rows, EXTRA), :], out[1], sems_out.at[1]),
        ]
    else:
        stores = [pltpu.make_async_copy(held, out[0], sems_out.at[0])]
    for copy in stores:
        copy.start()
    for copy in stores:
        copy.wait()


def assemble(places, blocks, rows, final):
    hbm = pl.BlockSpec(memory_space=pl.ANY)
    if final:
        shapes = [(4 * rows, WIDE), (EXTRA, WIDE)]
    else:
        shapes = [(4 * rows + EXTRA, WIDE)]
    return pl.pallas_call(
        functools.partial(assemble_kernel, rows, final),
        in_specs=[pl.BlockSpec(memory_space=pltpu.SMEM)] + [hbm] * 4,
        out_specs=[hbm] * len(shapes),
        out_shape=[jax.ShapeDtypeStruct(shape, BF) for shape in shapes],
        scratch_shapes=[
            pltpu.VMEM((4 * rows + EXTRA, WIDE), BF),
            pltpu.VMEM((4, EXTRA, WIDE), BF),
            pltpu.SemaphoreType.DMA((4,)),
            pltpu.SemaphoreType.DMA((4,)),
            pltpu.SemaphoreType.DMA((2,)),
        ],
        compiler_params=PARAMS,
        cost_estimate=COST,
        name="assemble",
    )(places, *blocks)


def together(*values):
    return lax.optimization_barrier(values)


def project(chunks, weights, total=None):
    for chunk, weight in zip(chunks, weights):
        term = jnp.dot(chunk, weight, preferred_element_type=F32)
        total = term if total is None else total + term
    return total


def state_kernel(cols_ref, key_ref, left_ref, right_ref, out_ref):
    for head, value_ref in enumerate((left_ref, right_ref)):
        weight = cols_ref[0, :, 4 + head : 5 + head]
        keys = key_ref[:, head * DQK : (head + 1) * DQK]
        scaled = (keys.astype(F32) * weight).astype(BF)
        out_ref[0, head] = lax.dot_general(
            scaled, value_ref[...], (((0,), (0,)), ((), ())), preferred_element_type=F32
        ).astype(BF)


def states(cols, key, value):
    parts = [pl.BlockSpec((ROWS, WIDE), lambda s, n=n: (s, n)) for n in (0, 0, 1)]
    return pl.pallas_call(
        state_kernel,
        grid=(2,),
        in_specs=[pl.BlockSpec((1, ROWS, 8), lambda s: (s, 0, 0)), *parts],
        out_specs=pl.BlockSpec((1, 2, DQK, DV), lambda s: (s, 0, 0, 0)),
        out_shape=jax.ShapeDtypeStruct((2, 2, DQK, DV), BF),
        compiler_params=SMALL,
        cost_estimate=COST,
        name="states",
    )(cols, key, value, value)


def intra_kernel(cols_ref, rows_ref, query_ref, key_ref, left_ref, right_ref, out_ref):
    segment = cols_ref[0, :, 6:7]
    segment_row = rows_ref[0, 4:5, :]
    for head, value_ref in enumerate((left_ref, right_ref)):
        cumul = cols_ref[0, :, head : head + 1]
        cumul_row = rows_ref[0, head : head + 1, :]
        gate_row = rows_ref[0, 2 + head : 3 + head, :]
        features = slice(head * DQK, (head + 1) * DQK)
        for start, size in ((0, 256), (256, 384)):
            reach = start + size
            scores = lax.dot_general(
                query_ref[start:reach, features],
                key_ref[:reach, features],
                (((1,), (1,)), ((), ())),
                preferred_element_type=F32,
            ) * (DQK**-0.5)
            later = start + lax.broadcasted_iota(jnp.int32, (size, reach), 0)
            earlier = lax.broadcasted_iota(jnp.int32, (size, reach), 1)
            keep = (later >= earlier) & (segment[start:reach] == segment_row[:, :reach])
            diff = cumul[start:reach] - cumul_row[:, :reach] + gate_row[:, :reach]
            mixed = (scores * jnp.exp(jnp.where(keep, diff, -1e30))).astype(BF)
            out_ref[start:reach, head * DV : (head + 1) * DV] = jnp.dot(
                mixed, value_ref[:reach, :], preferred_element_type=F32
            )


def intra(cols, rows, query, key, value):
    parts = [pl.BlockSpec((ROWS, WIDE), lambda s, n=n: (s, n)) for n in (0, 0, 0, 1)]
    return pl.pallas_call(
        intra_kernel,
        grid=(2,),
        in_specs=[
            pl.BlockSpec((1, ROWS, 8), lambda s: (s, 0, 0)),
            pl.BlockSpec((1, 8, ROWS), lambda s: (s, 0, 0)),
            *parts,
        ],
        out_specs=pl.BlockSpec((ROWS, 2 * DV), lambda s: (s, 0)),
        out_shape=jax.ShapeDtypeStruct((2 * ROWS, 2 * DV), F32),
        compiler_params=SMALL,
        cost_estimate=COST,
        name="intra",
    )(cols, rows, query, key, value, value)


def readout_kernel(cols_ref, query_ref, intra_ref, carried_ref, out_ref):
    head = pl.program_id(0)
    reach = jnp.where(head == 0, cols_ref[0, :, 2:3], cols_ref[0, :, 3:4])
    between = jnp.dot(query_ref[...], carried_ref[0], preferred_element_type=F32) * reach
    readout = intra_ref[...] + between
    scale = lax.rsqrt(jnp.mean(readout * readout, axis=-1, keepdims=True) + 1e-05)
    out_ref[...] = (readout * scale).astype(BF)


def readout(slot, cols, qkv, inner, carried):
    return pl.pallas_call(
        readout_kernel,
        grid=(2,),
        in_specs=[
            pl.BlockSpec((1, ROWS, 8), lambda h: (slot, 0, 0)),
            pl.BlockSpec((ROWS, DQK), lambda h: (slot, h)),
            pl.BlockSpec((ROWS, DV), lambda h: (slot, h)),
            pl.BlockSpec((1, DQK, DV), lambda h: (h, 0, 0)),
        ],
        out_specs=pl.BlockSpec((ROWS, DV), lambda h: (0, h)),
        out_shape=jax.ShapeDtypeStruct((ROWS, 2 * DV), BF),
        compiler_params=SMALL,
        cost_estimate=COST,
        name="readout",
    )(cols, qkv, inner, carried)


def join(decay, earlier, later):
    return (decay.astype(F32)[:, None, None] * earlier.astype(F32) + later.astype(F32)).astype(BF)


def times(left, right):
    return (left.astype(F32) * right.astype(F32)).astype(BF)


def pack(state, decay):
    tail = jnp.broadcast_to(decay[:, None, None], (2, 8, DV))
    return jnp.concatenate([state, tail], axis=1)


def unpack(message):
    return message[:, :-8], message[:, -1, 0]


def in_order(mine, axis, send):
    place = lax.axis_index(axis)
    blocks = [mine] + [shift(send(by), axis, by) for by in (1, 2, 3)]
    stacked = jnp.stack(blocks)
    return [lax.dynamic_index_in_dim(stacked, (place - j) % 4, 0, False) for j in range(4)]


def carry_in(decay, state, beside):
    x, z = lax.axis_index("x"), lax.axis_index("z")
    quarters = state.reshape(2, 4, DQK // 4, DV)

    def piece(by):
        return pack(lax.dynamic_index_in_dim(quarters, (x + by) % 4, 1, False), decay)

    line = [unpack(block) for block in in_order(piece(0), "x", piece)]
    prior = jnp.zeros_like(line[0][0])
    reach = jnp.ones_like(decay)
    priors, reaches = [], []
    for block, fade in line:
        priors.append(prior)
        reaches.append(reach)
        prior = join(fade, prior, block)
        reach = times(fade, reach)
    whole, done = together(pack(prior, reach), beside[0]())
    before = jnp.zeros_like(prior)
    for j, message in enumerate(in_order(whole, "z", lambda by: whole)):
        block, fade = unpack(message)
        before = jnp.where(j < z, join(fade, before, block), before)
    backs = jnp.stack([join(reaches[j], before, priors[j]) for j in range(4)])
    backs, done = together(backs, beside[1](done))

    def back(by):
        return lax.dynamic_index_in_dim(backs, (x + by) % 4, 0, False)

    inner = beside[2](done)
    carried, inner = together(jnp.stack(in_order(back(0), "x", back), axis=1), inner)
    return carried.reshape(2, DQK, DV), done, inner


def gate_rows(w_gates, core, place):
    gates = w_gates.T.reshape(2, 2, 2, OWN).transpose(1, 0, 2, 3).reshape(2, 4, OWN)
    mate = swap(gates)
    gates = jnp.where(
        core == 0,
        jnp.concatenate([gates[0], mate[0]], axis=1),
        jnp.concatenate([mate[1], gates[1]], axis=1),
    )
    gates = jnp.pad(gates.reshape(1, 4 * PIECE), ((0, 0), (0, WIDE - 4 * PIECE)))
    row = lax.broadcasted_iota(jnp.int32, (EXTRA, WIDE), 0)
    return jnp.where(row == place, gates, jnp.zeros_like(gates))


def per_device(tokens, w_query, w_key, w_value, w_gates, forget_bias, doc_lengths):
    core = lax.axis_index("core")
    y, z, x = lax.axis_index("y"), lax.axis_index("z"), lax.axis_index("x")
    chip = z * 4 + x
    last, middle = jnp.where(core == 0, x, z), jnp.where(core == 0, z, x)
    core_scalar = core[None].astype(jnp.int32)
    restore_places = jnp.concatenate([places(last), core_scalar])
    q_places = jnp.concatenate([places(middle), core_scalar])

    own = (w_query, w_key, w_value)
    mate = tuple(swap(weight) for weight in own)
    held, columns, rest = prepare(core_scalar, own, mate, gate_rows(w_gates, core, middle * 4 + y))
    rest = lax.all_gather(rest, ("y", "z", "x"), axis=0, tiled=True)
    tokens = together(tokens[0], held)[0]
    mate_tokens = swap(tokens)

    (held,) = assemble(places(y), together(*around(held, "yy")), PIECE, False)
    held, columns = together(held, columns)
    columns = weave(q_places, together(*around(columns, "zx")), False)
    held, region = assemble(places(middle), together(*around(held, "zx")), 4 * PIECE, True)
    columns = weave(restore_places, together(*around(columns, "xz")), True)
    regions = jnp.stack(together(*around(region, "xz")))
    regions = jnp.stack([lax.dynamic_index_in_dim(regions, (j - last) % 4, 0, False) for j in range(4)])
    regions = regions[:, :, : 4 * PIECE].reshape(4, 4, 4, 4, PIECE)
    w_gates = jnp.where(
        core == 0, regions.transpose(3, 2, 1, 0, 4), regions.transpose(3, 2, 0, 1, 4)
    ).reshape(4, 4096)
    w_gates = jnp.pad(w_gates, ((0, EXTRA - 4), (0, 0)))
    gates, normed, *chunks = normalize(
        jnp.concatenate([restore_places, places(y)]), tokens, mate_tokens, w_gates
    )
    chunks, by_y = chunks[:4], chunks[4:]
    gates = gates[:4].T
    gates = gates.reshape(2, ROWS, 4)
    lengths = doc_lengths[0]
    starts = jnp.cumsum(lengths) - lengths
    shard = chip * 2 + jnp.stack([core, 1 - core])
    positions = shard[:, None] * ROWS + jnp.arange(ROWS, dtype=jnp.int32)[None, :]
    resets = jnp.any(positions[:, :, None] == starts[None, None, :], axis=-1)
    bias = lax.dynamic_slice_in_dim(forget_bias, core * 2, 2)
    in_gate = gates[:, :, :2]
    cumul = jnp.cumsum(jax.nn.log_sigmoid(gates[:, :, 2:] + bias), axis=1)
    segment = jnp.cumsum(resets.astype(jnp.int32), axis=1)
    last = cumul[:, -1]
    same = (segment == segment[:, -1:])[:, :, None]
    weight = jnp.exp(jnp.where(same, last[:, None, :] - cumul + in_gate, -1e30))
    decay = (jnp.exp(last) * (segment[:, -1:] == 0).astype(F32)).astype(BF)
    reach = jnp.exp(cumul) * (segment == 0).astype(F32)[:, :, None] * (DQK**-0.5)
    seg = segment.astype(F32)[:, :, None]
    cols = jnp.concatenate([cumul, reach, weight, seg, jnp.zeros_like(seg)], axis=2)
    rows = jnp.concatenate([cumul, in_gate, seg, jnp.zeros_like(seg), weight], axis=2)
    rows = rows.transpose(0, 2, 1)

    key = project(chunks[:1], [held])
    held, columns, rest, key, cols, rows, decay = together(
        held, columns, rest, key, cols, rows, decay
    )
    blocks = around(held, "xz")
    columns = around(columns, "yy")
    value = jnp.dot(normed, rest, preferred_element_type=F32).astype(BF)
    key = project(chunks[1:], blocks[1:], key).astype(BF)
    state = states(cols, key, value)
    first = lax.dynamic_index_in_dim(state, core, 0, False)
    second = lax.dynamic_index_in_dim(state, 1 - core, 0, False)
    fade_first = lax.dynamic_index_in_dim(decay, core, 0, False)
    fade_second = lax.dynamic_index_in_dim(decay, 1 - core, 0, False)
    chip_state = join(fade_second, first, second)
    carried, query, inner = carry_in(
        times(fade_first, fade_second),
        chip_state,
        (
            lambda: project(by_y[:2], columns[:2]),
            lambda total: project(by_y[2:], columns[2:], total).astype(BF),
            lambda query: intra(cols, rows, query, key, value),
        ),
    )
    carried_second = join(fade_first, carried, first)
    mine = jnp.where(core == 0, carried, carried_second)
    other = jnp.where(core == 0, carried_second, carried)
    outgoing = readout(1, cols, query, inner, other)
    incoming = swap(outgoing)
    kept = readout(0, cols, query, inner, mine)
    result = jnp.where(
        core == 0,
        jnp.concatenate([kept, incoming], axis=1),
        jnp.concatenate([incoming, kept], axis=1),
    )
    return result.reshape(1, ROWS, 2048)


def solution(mesh):
    split = Mesh(mesh.devices.reshape(4, 4, 4, 2), ("y", "z", "x", "core"))
    weight_spec = P(("y", "z", "x", "core"), None)
    in_specs = (
        P("y", ("z", "x", "core"), None),
        weight_spec,
        weight_spec,
        weight_spec,
        weight_spec,
        P(),
        P("y", None),
    )
    out_specs = P("y", ("z", "x", "core"), None)
    return jax.shard_map(
        per_device, mesh=split, in_specs=in_specs, out_specs=out_specs, check_vma=False
    )
```

```python
import functools
import itertools

import jax
import jax.numpy as jnp
from jax import lax
from jax.experimental import pallas as pl
from jax.experimental.pallas import tpu as pltpu
from jax.sharding import Mesh, PartitionSpec as P

ROWS = 640
DQK = 256
DV = 512
OWN = 32
PIECE = 64
EXTRA = 16
WIDE = 512
BF = jnp.bfloat16
F32 = jnp.float32
COST = pl.CostEstimate(flops=0, bytes_accessed=1 << 10, transcendentals=0)
SMALL = pltpu.CompilerParams(vmem_limit_bytes=20 * 1024 * 1024)
LARGE = pltpu.CompilerParams(vmem_limit_bytes=60 * 1024 * 1024)
PARAMS = pltpu.CompilerParams(vmem_limit_bytes=20 * 1024 * 1024)


def swap(value):
    return lax.ppermute(value, "core", [(0, 1), (1, 0)])


def shift(value, axis, by):
    return lax.ppermute(value, axis, [(i, (i + by) % 4) for i in range(4)])


def hop(value, axes, by):
    names, pairs = ("y", "z", "x", "core"), []
    for source in itertools.product(range(4), range(4), range(4), range(2)):
        target = list(source)
        at = names.index(axes[source[3]])
        target[at] = (target[at] + by) % 4
        flat = [((p[0] * 4 + p[1]) * 4 + p[2]) * 2 + p[3] for p in (source, target)]
        pairs.append(tuple(flat))
    return lax.ppermute(value, names, pairs)


def around(value, axes):
    return (value,) + tuple(hop(value, axes, by) for by in (3, 2, 1))


def places(at):
    return jnp.stack([at, (at + 1) % 4, (at + 2) % 4, (at + 3) % 4]).astype(jnp.int32)


def normalize_kernel(places, own_ref, mate_ref, w_gates_ref, gates_ref, out_ref, *refs):
    chunks, by_y, scratch = refs[:4], refs[4:8], refs[8]
    raw = jnp.where(pl.program_id(0) == 0, own_ref[...], mate_ref[...])
    values = raw.astype(F32)
    scale = lax.rsqrt(jnp.mean(values * values, axis=-1, keepdims=True) + 1e-06)
    normed = (values * scale).astype(BF)
    out_ref[...] = normed
    gates_ref[...] = lax.dot_general(
        w_gates_ref[...], normed, (((1,), (1,)), ((), ())), preferred_element_type=F32
    )

    def reorder(last_step, other_step):
        for last in range(4):
            for other in range(4):
                for pair in range(2):
                    halves = []
                    for y in (2 * pair, 2 * pair + 1):
                        start = y * 1024 + last * last_step + other * other_step
                        halves.append(out_ref[:, start : start + 64])
                    start = last * 1024 + other * 256 + pair * 128
                    scratch[:, start : start + 128] = jnp.concatenate(halves, axis=1)

    pl.when(places[4] == 0)(lambda: reorder(64, 256))
    pl.when(places[4] == 1)(lambda: reorder(256, 64))
    for which in range(4):
        start = pl.multiple_of(places[which] * 1024, 1024)
        chunks[which][...] = scratch[:, pl.ds(start, 1024)]
        start = pl.multiple_of(places[5 + which] * 1024, 1024)
        by_y[which][...] = out_ref[:, pl.ds(start, 1024)]


def normalize(places, own, mate, w_gates):
    tile = 128
    steps = ROWS // tile
    return pl.pallas_call(
        normalize_kernel,
        grid_spec=pltpu.PrefetchScalarGridSpec(
            num_scalar_prefetch=1,
            grid=(2, steps),
            in_specs=[
                pl.BlockSpec((tile, 4096), lambda s, i, p: (jnp.where(s == 0, i, steps - 1), 0)),
                pl.BlockSpec((tile, 4096), lambda s, i, p: (jnp.where(s == 0, 0, i), 0)),
                pl.BlockSpec((EXTRA, 4096), lambda s, i, p: (0, 0)),
            ],
            out_specs=[pl.BlockSpec((EXTRA, tile), lambda s, i, p: (0, s * steps + i))]
            + [pl.BlockSpec((tile, 4096), lambda s, i, p: (s * steps + i, 0))]
            + [pl.BlockSpec((tile, 1024), lambda s, i, p: (s * steps + i, 0))] * 8,
            scratch_shapes=[pltpu.VMEM((tile, 4096), BF)],
        ),
        out_shape=[
            jax.ShapeDtypeStruct((EXTRA, 2 * ROWS), F32),
            jax.ShapeDtypeStruct((2 * ROWS, 4096), BF),
        ]
        + [jax.ShapeDtypeStruct((2 * ROWS, 1024), BF)] * 8,
        compiler_params=LARGE,
        cost_estimate=pl.CostEstimate(flops=0, bytes_accessed=32 << 20, transcendentals=0),
        name="normalize",
    )(places, own, mate, w_gates)


def prepare_kernel(
    core_ref, query, key, value, mate_query, mate_key, mate_value, region, held_ref, q_ref, rest_ref
):
    core = core_ref[0]
    narrow = pl.ds(pl.multiple_of(core * WIDE, WIDE), WIDE)
    wide = pl.ds(pl.multiple_of(core * 2 * WIDE, WIDE), 2 * WIDE)
    for source, rows in (((query, key, value), core), ((mate_query, mate_key, mate_value), 1 - core)):
        rows = pl.ds(pl.multiple_of(rows * OWN, OWN), OWN)
        q_ref[rows, :] = source[0][:, narrow]
        held_ref[rows, :] = source[1][:, narrow]
        rest_ref[rows, :] = source[2][:, wide]
    held_ref[PIECE:, :] = region[...]


def prepare(core, own, mate, region):
    vmem = pl.BlockSpec(memory_space=pltpu.VMEM)
    return pl.pallas_call(
        prepare_kernel,
        in_specs=[pl.BlockSpec(memory_space=pltpu.SMEM)] + [vmem] * 7,
        out_specs=[vmem] * 3,
        out_shape=[
            jax.ShapeDtypeStruct((PIECE + EXTRA, WIDE), BF),
            jax.ShapeDtypeStruct((PIECE, WIDE), BF),
            jax.ShapeDtypeStruct((PIECE, 2 * WIDE), BF),
        ],
        compiler_params=PARAMS,
        cost_estimate=COST,
        name="prepare",
    )(core, *own, *mate, region)


def weave_kernel(groups, places, *refs):
    blocks, out, held, sems_in, sem_out = refs[:4], *refs[4:]

    def run(target):
        copies = [
            pltpu.make_async_copy(block, target(places[which]), sems_in.at[which])
            for which, block in enumerate(blocks)
        ]
        for copy in copies:
            copy.start()
        for copy in copies:
            copy.wait()

    if groups:
        pl.when(places[4] == 0)(lambda: run(lambda place: held.at[:, place]))
        pl.when(places[4] == 1)(lambda: run(lambda place: held.at[place]))
    else:
        run(lambda place: held.at[place])
    store = pltpu.make_async_copy(held, out, sem_out)
    store.start()
    store.wait()


def weave(places, blocks, groups):
    hbm = pl.BlockSpec(memory_space=pl.ANY)
    shape = (4, 4, PIECE, WIDE) if groups else (4, PIECE, WIDE)
    blocks = [block.reshape(shape[1:]) for block in blocks]
    return pl.pallas_call(
        functools.partial(weave_kernel, groups),
        in_specs=[pl.BlockSpec(memory_space=pltpu.SMEM)] + [hbm] * 4,
        out_specs=hbm,
        out_shape=jax.ShapeDtypeStruct(shape, BF),
        scratch_shapes=[
            pltpu.VMEM(shape, BF),
            pltpu.SemaphoreType.DMA((4,)),
            pltpu.SemaphoreType.DMA,
        ],
        compiler_params=PARAMS,
        cost_estimate=COST,
        name="weave",
    )(places, *blocks).reshape(-1, WIDE)


def assemble_kernel(rows, final, places, *refs):
    blocks, out, held, regions, sems_in, sems_more, sems_out = refs[:4], refs[4:-5], *refs[-5:]
    loads, extras = [], []
    for which, block in enumerate(blocks):
        start = pl.multiple_of(places[which] * rows, PIECE)
        loads.append(
            pltpu.make_async_copy(
                block.at[pl.ds(0, rows), :], held.at[pl.ds(start, rows), :], sems_in.at[which]
            )
        )
        extras.append(
            pltpu.make_async_copy(
                block.at[pl.ds(rows, EXTRA), :], regions.at[which], sems_more.at[which]
            )
        )
    for copy in extras + loads:
        copy.start()
    for copy in extras:
        copy.wait()
    held[4 * rows :, :] = (regions[0] + regions[1]) + (regions[2] + regions[3])
    for copy in loads:
        copy.wait()
    if final:
        stores = [
            pltpu.make_async_copy(held.at[pl.ds(0, 4 * rows), :], out[0], sems_out.at[0]),
            pltpu.make_async_copy(held.at[pl.ds(4 * rows, EXTRA), :], out[1], sems_out.at[1]),
        ]
    else:
        stores = [pltpu.make_async_copy(held, out[0], sems_out.at[0])]
    for copy in stores:
        copy.start()
    for copy in stores:
        copy.wait()


def assemble(places, blocks, rows, final):
    hbm = pl.BlockSpec(memory_space=pl.ANY)
    if final:
        shapes = [(4 * rows, WIDE), (EXTRA, WIDE)]
    else:
        shapes = [(4 * rows + EXTRA, WIDE)]
    return pl.pallas_call(
        functools.partial(assemble_kernel, rows, final),
        in_specs=[pl.BlockSpec(memory_space=pltpu.SMEM)] + [hbm] * 4,
        out_specs=[hbm] * len(shapes),
        out_shape=[jax.ShapeDtypeStruct(shape, BF) for shape in shapes],
        scratch_shapes=[
            pltpu.VMEM((4 * rows + EXTRA, WIDE), BF),
            pltpu.VMEM((4, EXTRA, WIDE), BF),
            pltpu.SemaphoreType.DMA((4,)),
            pltpu.SemaphoreType.DMA((4,)),
            pltpu.SemaphoreType.DMA((2,)),
        ],
        compiler_params=PARAMS,
        cost_estimate=COST,
        name="assemble",
    )(places, *blocks)


def together(*values):
    return lax.optimization_barrier(values)


def project(chunks, weights, total=None):
    for chunk, weight in zip(chunks, weights):
        term = jnp.dot(chunk, weight, preferred_element_type=F32)
        total = term if total is None else total + term
    return total


def state_kernel(cols_ref, key_ref, left_ref, right_ref, out_ref):
    for head, value_ref in enumerate((left_ref, right_ref)):
        weight = cols_ref[0, :, 4 + head : 5 + head]
        keys = key_ref[:, head * DQK : (head + 1) * DQK]
        scaled = (keys.astype(F32) * weight).astype(BF)
        out_ref[0, head] = lax.dot_general(
            scaled, value_ref[...], (((0,), (0,)), ((), ())), preferred_element_type=F32
        ).astype(BF)


def states(cols, key, value):
    parts = [pl.BlockSpec((ROWS, WIDE), lambda s, n=n: (s, n)) for n in (0, 0, 1)]
    return pl.pallas_call(
        state_kernel,
        grid=(2,),
        in_specs=[pl.BlockSpec((1, ROWS, 8), lambda s: (s, 0, 0)), *parts],
        out_specs=pl.BlockSpec((1, 2, DQK, DV), lambda s: (s, 0, 0, 0)),
        out_shape=jax.ShapeDtypeStruct((2, 2, DQK, DV), BF),
        compiler_params=SMALL,
        cost_estimate=COST,
        name="states",
    )(cols, key, value, value)


def intra_kernel(cols_ref, rows_ref, query_ref, key_ref, left_ref, right_ref, out_ref):
    segment = cols_ref[0, :, 6:7]
    segment_row = rows_ref[0, 4:5, :]
    for head, value_ref in enumerate((left_ref, right_ref)):
        cumul = cols_ref[0, :, head : head + 1]
        cumul_row = rows_ref[0, head : head + 1, :]
        gate_row = rows_ref[0, 2 + head : 3 + head, :]
        features = slice(head * DQK, (head + 1) * DQK)
        for start, size in ((0, 256), (256, 384)):
            reach = start + size
            scores = lax.dot_general(
                query_ref[start:reach, features],
                key_ref[:reach, features],
                (((1,), (1,)), ((), ())),
                preferred_element_type=F32,
            ) * (DQK**-0.5)
            later = start + lax.broadcasted_iota(jnp.int32, (size, reach), 0)
            earlier = lax.broadcasted_iota(jnp.int32, (size, reach), 1)
            keep = (later >= earlier) & (segment[start:reach] == segment_row[:, :reach])
            diff = cumul[start:reach] - cumul_row[:, :reach] + gate_row[:, :reach]
            mixed = (scores * jnp.exp(jnp.where(keep, diff, -1e30))).astype(BF)
            out_ref[start:reach, head * DV : (head + 1) * DV] = jnp.dot(
                mixed, value_ref[:reach, :], preferred_element_type=F32
            )


def intra(cols, rows, query, key, value):
    parts = [pl.BlockSpec((ROWS, WIDE), lambda s, n=n: (s, n)) for n in (0, 0, 0, 1)]
    return pl.pallas_call(
        intra_kernel,
        grid=(2,),
        in_specs=[
            pl.BlockSpec((1, ROWS, 8), lambda s: (s, 0, 0)),
            pl.BlockSpec((1, 8, ROWS), lambda s: (s, 0, 0)),
            *parts,
        ],
        out_specs=pl.BlockSpec((ROWS, 2 * DV), lambda s: (s, 0)),
        out_shape=jax.ShapeDtypeStruct((2 * ROWS, 2 * DV), F32),
        compiler_params=SMALL,
        cost_estimate=COST,
        name="intra",
    )(cols, rows, query, key, value, value)


def readout_kernel(cols_ref, query_ref, intra_ref, carried_ref, out_ref):
    head = pl.program_id(0)
    reach = jnp.where(head == 0, cols_ref[0, :, 2:3], cols_ref[0, :, 3:4])
    between = jnp.dot(query_ref[...], carried_ref[0], preferred_element_type=F32) * reach
    readout = intra_ref[...] + between
    scale = lax.rsqrt(jnp.mean(readout * readout, axis=-1, keepdims=True) + 1e-05)
    out_ref[...] = (readout * scale).astype(BF)


def readout(slot, cols, qkv, inner, carried):
    return pl.pallas_call(
        readout_kernel,
        grid=(2,),
        in_specs=[
            pl.BlockSpec((1, ROWS, 8), lambda h: (slot, 0, 0)),
            pl.BlockSpec((ROWS, DQK), lambda h: (slot, h)),
            pl.BlockSpec((ROWS, DV), lambda h: (slot, h)),
            pl.BlockSpec((1, DQK, DV), lambda h: (h, 0, 0)),
        ],
        out_specs=pl.BlockSpec((ROWS, DV), lambda h: (0, h)),
        out_shape=jax.ShapeDtypeStruct((ROWS, 2 * DV), BF),
        compiler_params=SMALL,
        cost_estimate=COST,
        name="readout",
    )(cols, qkv, inner, carried)


def join(decay, earlier, later):
    return (decay.astype(F32)[:, None, None] * earlier.astype(F32) + later.astype(F32)).astype(BF)


def times(left, right):
    return (left.astype(F32) * right.astype(F32)).astype(BF)


def pack(state, decay):
    tail = jnp.broadcast_to(decay[:, None, None], (2, 8, DV))
    return jnp.concatenate([state, tail], axis=1)


def unpack(message):
    return message[:, :-8], message[:, -1, 0]


def in_order(mine, axis, send):
    place = lax.axis_index(axis)
    blocks = [mine] + [shift(send(by), axis, by) for by in (1, 2, 3)]
    stacked = jnp.stack(blocks)
    return [lax.dynamic_index_in_dim(stacked, (place - j) % 4, 0, False) for j in range(4)]


def carry_in(decay, state, beside):
    x, z = lax.axis_index("x"), lax.axis_index("z")
    quarters = state.reshape(2, 4, DQK // 4, DV)

    def piece(by):
        return pack(lax.dynamic_index_in_dim(quarters, (x + by) % 4, 1, False), decay)

    line = [unpack(block) for block in in_order(piece(0), "x", piece)]
    prior = jnp.zeros_like(line[0][0])
    reach = jnp.ones_like(decay)
    priors, reaches = [], []
    for block, fade in line:
        priors.append(prior)
        reaches.append(reach)
        prior = join(fade, prior, block)
        reach = times(fade, reach)
    whole, done = together(pack(prior, reach), beside[0]())
    before = jnp.zeros_like(prior)
    for j, message in enumerate(in_order(whole, "z", lambda by: whole)):
        block, fade = unpack(message)
        before = jnp.where(j < z, join(fade, before, block), before)
    backs = jnp.stack([join(reaches[j], before, priors[j]) for j in range(4)])
    backs, done = together(backs, beside[1](done))

    def back(by):
        return lax.dynamic_index_in_dim(backs, (x + by) % 4, 0, False)

    inner = beside[2](done)
    carried, inner = together(jnp.stack(in_order(back(0), "x", back), axis=1), inner)
    return carried.reshape(2, DQK, DV), done, inner


def gate_rows(w_gates, core, place):
    gates = w_gates.T.reshape(2, 2, 2, OWN).transpose(1, 0, 2, 3).reshape(2, 4, OWN)
    mate = swap(gates)
    gates = jnp.where(
        core == 0,
        jnp.concatenate([gates[0], mate[0]], axis=1),
        jnp.concatenate([mate[1], gates[1]], axis=1),
    )
    gates = jnp.pad(gates.reshape(1, 4 * PIECE), ((0, 0), (0, WIDE - 4 * PIECE)))
    row = lax.broadcasted_iota(jnp.int32, (EXTRA, WIDE), 0)
    return jnp.where(row == place, gates, jnp.zeros_like(gates))


def per_device(tokens, w_query, w_key, w_value, w_gates, forget_bias, doc_lengths):
    core = lax.axis_index("core")
    y, z, x = lax.axis_index("y"), lax.axis_index("z"), lax.axis_index("x")
    chip = z * 4 + x
    last, middle = jnp.where(core == 0, x, z), jnp.where(core == 0, z, x)
    core_scalar = core[None].astype(jnp.int32)
    restore_places = jnp.concatenate([places(last), core_scalar])
    q_places = jnp.concatenate([places(middle), core_scalar])

    own = (w_query, w_key, w_value)
    mate = tuple(swap(weight) for weight in own)
    held, columns, rest = prepare(core_scalar, own, mate, gate_rows(w_gates, core, middle * 4 + y))
    rest = lax.all_gather(rest, ("y", "z", "x"), axis=0, tiled=True)
    tokens = together(tokens[0], held)[0]
    mate_tokens = swap(tokens)

    (held,) = assemble(places(y), together(*around(held, "yy")), PIECE, False)
    held, columns = together(held, columns)
    columns = weave(q_places, together(*around(columns, "zx")), False)
    held, region = assemble(places(middle), together(*around(held, "zx")), 4 * PIECE, True)
    columns = weave(restore_places, together(*around(columns, "xz")), True)
    regions = jnp.stack(together(*around(region, "xz")))
    regions = jnp.stack([lax.dynamic_index_in_dim(regions, (j - last) % 4, 0, False) for j in range(4)])
    regions = regions[:, :, : 4 * PIECE].reshape(4, 4, 4, 4, PIECE)
    w_gates = jnp.where(
        core == 0, regions.transpose(3, 2, 1, 0, 4), regions.transpose(3, 2, 0, 1, 4)
    ).reshape(4, 4096)
    w_gates = jnp.pad(w_gates, ((0, EXTRA - 4), (0, 0)))
    gates, normed, *chunks = normalize(
        jnp.concatenate([restore_places, places(y)]), tokens, mate_tokens, w_gates
    )
    chunks, by_y = chunks[:4], chunks[4:]
    gates = gates[:4].T
    gates = gates.reshape(2, ROWS, 4)
    lengths = doc_lengths[0]
    starts = jnp.cumsum(lengths) - lengths
    shard = chip * 2 + jnp.stack([core, 1 - core])
    positions = shard[:, None] * ROWS + jnp.arange(ROWS, dtype=jnp.int32)[None, :]
    resets = jnp.any(positions[:, :, None] == starts[None, None, :], axis=-1)
    bias = lax.dynamic_slice_in_dim(forget_bias, core * 2, 2)
    in_gate = gates[:, :, :2]
    cumul = jnp.cumsum(jax.nn.log_sigmoid(gates[:, :, 2:] + bias), axis=1)
    segment = jnp.cumsum(resets.astype(jnp.int32), axis=1)
    last = cumul[:, -1]
    same = (segment == segment[:, -1:])[:, :, None]
    weight = jnp.exp(jnp.where(same, last[:, None, :] - cumul + in_gate, -1e30))
    decay = (jnp.exp(last) * (segment[:, -1:] == 0).astype(F32)).astype(BF)
    reach = jnp.exp(cumul) * (segment == 0).astype(F32)[:, :, None] * (DQK**-0.5)
    seg = segment.astype(F32)[:, :, None]
    cols = jnp.concatenate([cumul, reach, weight, seg, jnp.zeros_like(seg)], axis=2)
    rows = jnp.concatenate([cumul, in_gate, seg, jnp.zeros_like(seg), weight], axis=2)
    rows = rows.transpose(0, 2, 1)

    key = project(chunks[:1], [held])
    query = project(by_y[:1], [columns])
    held, columns, rest, key, query, cols, rows, decay = together(
        held, columns, rest, key, query, cols, rows, decay
    )
    blocks = around(held, "xz")
    columns = around(columns, "yy")
    value = jnp.dot(normed, rest, preferred_element_type=F32).astype(BF)
    key = project(chunks[1:], blocks[1:], key).astype(BF)
    state = states(cols, key, value)
    first = lax.dynamic_index_in_dim(state, core, 0, False)
    second = lax.dynamic_index_in_dim(state, 1 - core, 0, False)
    fade_first = lax.dynamic_index_in_dim(decay, core, 0, False)
    fade_second = lax.dynamic_index_in_dim(decay, 1 - core, 0, False)
    chip_state = join(fade_second, first, second)
    carried, query, inner = carry_in(
        times(fade_first, fade_second),
        chip_state,
        (
            lambda: (project(by_y[1:2], columns[1:2], query), by_y[2], by_y[3]),
            lambda done: project(done[1:], columns[2:], done[0]).astype(BF),
            lambda query: intra(cols, rows, query, key, value),
        ),
    )
    carried_second = join(fade_first, carried, first)
    mine = jnp.where(core == 0, carried, carried_second)
    other = jnp.where(core == 0, carried_second, carried)
    outgoing = readout(1, cols, query, inner, other)
    incoming = swap(outgoing)
    kept = readout(0, cols, query, inner, mine)
    result = jnp.where(
        core == 0,
        jnp.concatenate([kept, incoming], axis=1),
        jnp.concatenate([incoming, kept], axis=1),
    )
    return result.reshape(1, ROWS, 2048)


def solution(mesh):
    split = Mesh(mesh.devices.reshape(4, 4, 4, 2), ("y", "z", "x", "core"))
    weight_spec = P(("y", "z", "x", "core"), None)
    in_specs = (
        P("y", ("z", "x", "core"), None),
        weight_spec,
        weight_spec,
        weight_spec,
        weight_spec,
        P(),
        P("y", None),
    )
    out_specs = P("y", ("z", "x", "core"), None)
    return jax.shard_map(
        per_device, mesh=split, in_specs=in_specs, out_specs=out_specs, check_vma=False
    )
```

```python
import functools
import itertools

import jax
import jax.numpy as jnp
from jax import lax
from jax.experimental import pallas as pl
from jax.experimental.pallas import tpu as pltpu
from jax.sharding import Mesh, PartitionSpec as P

ROWS = 640
DQK = 256
DV = 512
OWN = 32
PIECE = 64
EXTRA = 16
WIDE = 512
BF = jnp.bfloat16
F32 = jnp.float32
COST = pl.CostEstimate(flops=0, bytes_accessed=1 << 10, transcendentals=0)
SMALL = pltpu.CompilerParams(vmem_limit_bytes=20 * 1024 * 1024)
LARGE = pltpu.CompilerParams(vmem_limit_bytes=60 * 1024 * 1024)
PARAMS = pltpu.CompilerParams(vmem_limit_bytes=20 * 1024 * 1024)


def swap(value):
    return lax.ppermute(value, "core", [(0, 1), (1, 0)])


def shift(value, axis, by):
    return lax.ppermute(value, axis, [(i, (i + by) % 4) for i in range(4)])


def hop(value, axes, by):
    names, pairs = ("y", "z", "x", "core"), []
    for source in itertools.product(range(4), range(4), range(4), range(2)):
        target = list(source)
        at = names.index(axes[source[3]])
        target[at] = (target[at] + by) % 4
        flat = [((p[0] * 4 + p[1]) * 4 + p[2]) * 2 + p[3] for p in (source, target)]
        pairs.append(tuple(flat))
    return lax.ppermute(value, names, pairs)


def around(value, axes):
    return (value,) + tuple(hop(value, axes, by) for by in (3, 2, 1))


def places(at):
    return jnp.stack([at, (at + 1) % 4, (at + 2) % 4, (at + 3) % 4]).astype(jnp.int32)


def normalize_kernel(places, own_ref, mate_ref, w_gates_ref, gates_ref, out_ref, *refs):
    chunks, by_y, scratch = refs[:4], refs[4:8], refs[8]
    raw = jnp.where(pl.program_id(0) == 0, own_ref[...], mate_ref[...])
    values = raw.astype(F32)
    scale = lax.rsqrt(jnp.mean(values * values, axis=-1, keepdims=True) + 1e-06)
    normed = (values * scale).astype(BF)
    out_ref[...] = normed
    gates_ref[...] = lax.dot_general(
        w_gates_ref[...], normed, (((1,), (1,)), ((), ())), preferred_element_type=F32
    )

    def reorder(last_step, other_step):
        for last in range(4):
            for other in range(4):
                for pair in range(2):
                    halves = []
                    for y in (2 * pair, 2 * pair + 1):
                        start = y * 1024 + last * last_step + other * other_step
                        halves.append(out_ref[:, start : start + 64])
                    start = last * 1024 + other * 256 + pair * 128
                    scratch[:, start : start + 128] = jnp.concatenate(halves, axis=1)

    pl.when(places[4] == 0)(lambda: reorder(64, 256))
    pl.when(places[4] == 1)(lambda: reorder(256, 64))
    for which in range(4):
        start = pl.multiple_of(places[which] * 1024, 1024)
        chunks[which][...] = scratch[:, pl.ds(start, 1024)]
        start = pl.multiple_of(places[5 + which] * 1024, 1024)
        by_y[which][...] = out_ref[:, pl.ds(start, 1024)]


def normalize(places, own, mate, w_gates):
    tile = 128
    steps = ROWS // tile
    return pl.pallas_call(
        normalize_kernel,
        grid_spec=pltpu.PrefetchScalarGridSpec(
            num_scalar_prefetch=1,
            grid=(2, steps),
            in_specs=[
                pl.BlockSpec((tile, 4096), lambda s, i, p: (jnp.where(s == 0, i, steps - 1), 0)),
                pl.BlockSpec((tile, 4096), lambda s, i, p: (jnp.where(s == 0, 0, i), 0)),
                pl.BlockSpec((EXTRA, 4096), lambda s, i, p: (0, 0)),
            ],
            out_specs=[pl.BlockSpec((EXTRA, tile), lambda s, i, p: (0, s * steps + i))]
            + [pl.BlockSpec((tile, 4096), lambda s, i, p: (s * steps + i, 0))]
            + [pl.BlockSpec((tile, 1024), lambda s, i, p: (s * steps + i, 0))] * 8,
            scratch_shapes=[pltpu.VMEM((tile, 4096), BF)],
        ),
        out_shape=[
            jax.ShapeDtypeStruct((EXTRA, 2 * ROWS), F32),
            jax.ShapeDtypeStruct((2 * ROWS, 4096), BF),
        ]
        + [jax.ShapeDtypeStruct((2 * ROWS, 1024), BF)] * 8,
        compiler_params=LARGE,
        cost_estimate=pl.CostEstimate(flops=0, bytes_accessed=32 << 20, transcendentals=0),
        name="normalize",
    )(places, own, mate, w_gates)


def prepare_values_kernel(core_ref, value, mate_value, rest_ref):
    core = core_ref[0]
    wide = pl.ds(pl.multiple_of(core * 2 * WIDE, WIDE), 2 * WIDE)
    for source, rows in ((value, core), (mate_value, 1 - core)):
        rest_ref[pl.ds(pl.multiple_of(rows * OWN, OWN), OWN), :] = source[:, wide]


def prepare_values(core, own, mate):
    vmem = pl.BlockSpec(memory_space=pltpu.VMEM)
    return pl.pallas_call(
        prepare_values_kernel,
        in_specs=[pl.BlockSpec(memory_space=pltpu.SMEM)] + [vmem] * 2,
        out_specs=vmem,
        out_shape=jax.ShapeDtypeStruct((PIECE, 2 * WIDE), BF),
        compiler_params=LARGE,
        cost_estimate=COST,
        name="prepare_values",
    )(core, own, mate)


def prepare_kernel(core_ref, query, key, mate_query, mate_key, region, held_ref, q_ref):
    core = core_ref[0]
    narrow = pl.ds(pl.multiple_of(core * WIDE, WIDE), WIDE)
    for queries, keys, rows in ((query, key, core), (mate_query, mate_key, 1 - core)):
        rows = pl.ds(pl.multiple_of(rows * OWN, OWN), OWN)
        q_ref[rows, :] = queries[:, narrow]
        held_ref[rows, :] = keys[:, narrow]
    held_ref[PIECE:, :] = region[...]


def prepare(core, own, mate, region):
    vmem = pl.BlockSpec(memory_space=pltpu.VMEM)
    return pl.pallas_call(
        prepare_kernel,
        in_specs=[pl.BlockSpec(memory_space=pltpu.SMEM)] + [vmem] * 5,
        out_specs=[vmem] * 2,
        out_shape=[
            jax.ShapeDtypeStruct((PIECE + EXTRA, WIDE), BF),
            jax.ShapeDtypeStruct((PIECE, WIDE), BF),
        ],
        compiler_params=LARGE,
        cost_estimate=COST,
        name="prepare",
    )(core, *own, *mate, region)


def weave_kernel(groups, places, *refs):
    blocks, out, held, sems_in, sem_out = refs[:4], *refs[4:]

    def run(target):
        copies = [
            pltpu.make_async_copy(block, target(places[which]), sems_in.at[which])
            for which, block in enumerate(blocks)
        ]
        for copy in copies:
            copy.start()
        for copy in copies:
            copy.wait()

    if groups:
        pl.when(places[4] == 0)(lambda: run(lambda place: held.at[:, place]))
        pl.when(places[4] == 1)(lambda: run(lambda place: held.at[place]))
    else:
        run(lambda place: held.at[place])
    store = pltpu.make_async_copy(held, out, sem_out)
    store.start()
    store.wait()


def weave(places, blocks, groups):
    hbm = pl.BlockSpec(memory_space=pl.ANY)
    shape = (4, 4, PIECE, WIDE) if groups else (4, PIECE, WIDE)
    blocks = [block.reshape(shape[1:]) for block in blocks]
    return pl.pallas_call(
        functools.partial(weave_kernel, groups),
        in_specs=[pl.BlockSpec(memory_space=pltpu.SMEM)] + [hbm] * 4,
        out_specs=hbm,
        out_shape=jax.ShapeDtypeStruct(shape, BF),
        scratch_shapes=[
            pltpu.VMEM(shape, BF),
            pltpu.SemaphoreType.DMA((4,)),
            pltpu.SemaphoreType.DMA,
        ],
        compiler_params=PARAMS,
        cost_estimate=COST,
        name="weave",
    )(places, *blocks).reshape(-1, WIDE)


def assemble_kernel(rows, final, places, *refs):
    blocks, out, held, regions, sems_in, sems_more, sems_out = refs[:4], refs[4:-5], *refs[-5:]
    loads, extras = [], []
    for which, block in enumerate(blocks):
        start = pl.multiple_of(places[which] * rows, PIECE)
        loads.append(
            pltpu.make_async_copy(
                block.at[pl.ds(0, rows), :], held.at[pl.ds(start, rows), :], sems_in.at[which]
            )
        )
        extras.append(
            pltpu.make_async_copy(
                block.at[pl.ds(rows, EXTRA), :], regions.at[which], sems_more.at[which]
            )
        )
    for copy in extras + loads:
        copy.start()
    for copy in extras:
        copy.wait()
    held[4 * rows :, :] = (regions[0] + regions[1]) + (regions[2] + regions[3])
    for copy in loads:
        copy.wait()
    if final:
        stores = [
            pltpu.make_async_copy(held.at[pl.ds(0, 4 * rows), :], out[0], sems_out.at[0]),
            pltpu.make_async_copy(held.at[pl.ds(4 * rows, EXTRA), :], out[1], sems_out.at[1]),
        ]
    else:
        stores = [pltpu.make_async_copy(held, out[0], sems_out.at[0])]
    for copy in stores:
        copy.start()
    for copy in stores:
        copy.wait()


def assemble(places, blocks, rows, final):
    hbm = pl.BlockSpec(memory_space=pl.ANY)
    if final:
        shapes = [(4 * rows, WIDE), (EXTRA, WIDE)]
    else:
        shapes = [(4 * rows + EXTRA, WIDE)]
    return pl.pallas_call(
        functools.partial(assemble_kernel, rows, final),
        in_specs=[pl.BlockSpec(memory_space=pltpu.SMEM)] + [hbm] * 4,
        out_specs=[hbm] * len(shapes),
        out_shape=[jax.ShapeDtypeStruct(shape, BF) for shape in shapes],
        scratch_shapes=[
            pltpu.VMEM((4 * rows + EXTRA, WIDE), BF),
            pltpu.VMEM((4, EXTRA, WIDE), BF),
            pltpu.SemaphoreType.DMA((4,)),
            pltpu.SemaphoreType.DMA((4,)),
            pltpu.SemaphoreType.DMA((2,)),
        ],
        compiler_params=PARAMS,
        cost_estimate=COST,
        name="assemble",
    )(places, *blocks)


def together(*values):
    return lax.optimization_barrier(values)


def project(chunks, weights, total=None):
    for chunk, weight in zip(chunks, weights):
        term = jnp.dot(chunk, weight, preferred_element_type=F32)
        total = term if total is None else total + term
    return total


def state_kernel(cols_ref, key_ref, left_ref, right_ref, out_ref):
    for head, value_ref in enumerate((left_ref, right_ref)):
        weight = cols_ref[0, :, 4 + head : 5 + head]
        keys = key_ref[:, head * DQK : (head + 1) * DQK]
        scaled = (keys.astype(F32) * weight).astype(BF)
        out_ref[0, head] = lax.dot_general(
            scaled, value_ref[...], (((0,), (0,)), ((), ())), preferred_element_type=F32
        ).astype(BF)


def states(cols, key, value):
    parts = [pl.BlockSpec((ROWS, WIDE), lambda s, n=n: (s, n)) for n in (0, 0, 1)]
    return pl.pallas_call(
        state_kernel,
        grid=(2,),
        in_specs=[pl.BlockSpec((1, ROWS, 8), lambda s: (s, 0, 0)), *parts],
        out_specs=pl.BlockSpec((1, 2, DQK, DV), lambda s: (s, 0, 0, 0)),
        out_shape=jax.ShapeDtypeStruct((2, 2, DQK, DV), BF),
        compiler_params=SMALL,
        cost_estimate=COST,
        name="states",
    )(cols, key, value, value)


def intra_kernel(cols_ref, rows_ref, query_ref, key_ref, left_ref, right_ref, out_ref):
    segment = cols_ref[0, :, 6:7]
    segment_row = rows_ref[0, 4:5, :]
    for head, value_ref in enumerate((left_ref, right_ref)):
        cumul = cols_ref[0, :, head : head + 1]
        cumul_row = rows_ref[0, head : head + 1, :]
        gate_row = rows_ref[0, 2 + head : 3 + head, :]
        features = slice(head * DQK, (head + 1) * DQK)
        for start, size in ((0, 256), (256, 384)):
            reach = start + size
            scores = lax.dot_general(
                query_ref[start:reach, features],
                key_ref[:reach, features],
                (((1,), (1,)), ((), ())),
                preferred_element_type=F32,
            ) * (DQK**-0.5)
            later = start + lax.broadcasted_iota(jnp.int32, (size, reach), 0)
            earlier = lax.broadcasted_iota(jnp.int32, (size, reach), 1)
            keep = (later >= earlier) & (segment[start:reach] == segment_row[:, :reach])
            diff = cumul[start:reach] - cumul_row[:, :reach] + gate_row[:, :reach]
            mixed = (scores * jnp.exp(jnp.where(keep, diff, -1e30))).astype(BF)
            out_ref[start:reach, head * DV : (head + 1) * DV] = jnp.dot(
                mixed, value_ref[:reach, :], preferred_element_type=F32
            )


def intra(cols, rows, query, key, value):
    parts = [pl.BlockSpec((ROWS, WIDE), lambda s, n=n: (s, n)) for n in (0, 0, 0, 1)]
    return pl.pallas_call(
        intra_kernel,
        grid=(2,),
        in_specs=[
            pl.BlockSpec((1, ROWS, 8), lambda s: (s, 0, 0)),
            pl.BlockSpec((1, 8, ROWS), lambda s: (s, 0, 0)),
            *parts,
        ],
        out_specs=pl.BlockSpec((ROWS, 2 * DV), lambda s: (s, 0)),
        out_shape=jax.ShapeDtypeStruct((2 * ROWS, 2 * DV), F32),
        compiler_params=SMALL,
        cost_estimate=COST,
        name="intra",
    )(cols, rows, query, key, value, value)


def readout_kernel(cols_ref, query_ref, intra_ref, carried_ref, out_ref):
    head = pl.program_id(0)
    reach = jnp.where(head == 0, cols_ref[0, :, 2:3], cols_ref[0, :, 3:4])
    between = jnp.dot(query_ref[...], carried_ref[0], preferred_element_type=F32) * reach
    readout = intra_ref[...] + between
    scale = lax.rsqrt(jnp.mean(readout * readout, axis=-1, keepdims=True) + 1e-05)
    out_ref[...] = (readout * scale).astype(BF)


def readout(slot, cols, qkv, inner, carried):
    return pl.pallas_call(
        readout_kernel,
        grid=(2,),
        in_specs=[
            pl.BlockSpec((1, ROWS, 8), lambda h: (slot, 0, 0)),
            pl.BlockSpec((ROWS, DQK), lambda h: (slot, h)),
            pl.BlockSpec((ROWS, DV), lambda h: (slot, h)),
            pl.BlockSpec((1, DQK, DV), lambda h: (h, 0, 0)),
        ],
        out_specs=pl.BlockSpec((ROWS, DV), lambda h: (0, h)),
        out_shape=jax.ShapeDtypeStruct((ROWS, 2 * DV), BF),
        compiler_params=SMALL,
        cost_estimate=COST,
        name="readout",
    )(cols, qkv, inner, carried)


def join(decay, earlier, later):
    return (decay.astype(F32)[:, None, None] * earlier.astype(F32) + later.astype(F32)).astype(BF)


def times(left, right):
    return (left.astype(F32) * right.astype(F32)).astype(BF)


def pack(state, decay):
    tail = jnp.broadcast_to(decay[:, None, None], (2, 8, DV))
    return jnp.concatenate([state, tail], axis=1)


def unpack(message):
    return message[:, :-8], message[:, -1, 0]


def in_order(mine, axis, send):
    place = lax.axis_index(axis)
    blocks = [mine] + [shift(send(by), axis, by) for by in (1, 2, 3)]
    stacked = jnp.stack(blocks)
    return [lax.dynamic_index_in_dim(stacked, (place - j) % 4, 0, False) for j in range(4)]


def carry_in(decay, state, beside):
    x, z = lax.axis_index("x"), lax.axis_index("z")
    quarters = state.reshape(2, 4, DQK // 4, DV)

    def piece(by):
        return pack(lax.dynamic_index_in_dim(quarters, (x + by) % 4, 1, False), decay)

    line = [unpack(block) for block in in_order(piece(0), "x", piece)]
    prior = jnp.zeros_like(line[0][0])
    reach = jnp.ones_like(decay)
    priors, reaches = [], []
    for block, fade in line:
        priors.append(prior)
        reaches.append(reach)
        prior = join(fade, prior, block)
        reach = times(fade, reach)
    whole, done = together(pack(prior, reach), beside[0]())
    before = jnp.zeros_like(prior)
    for j, message in enumerate(in_order(whole, "z", lambda by: whole)):
        block, fade = unpack(message)
        before = jnp.where(j < z, join(fade, before, block), before)
    backs = jnp.stack([join(reaches[j], before, priors[j]) for j in range(4)])
    backs, done = together(backs, beside[1](done))

    def back(by):
        return lax.dynamic_index_in_dim(backs, (x + by) % 4, 0, False)

    inner = beside[2](done)
    carried, inner = together(jnp.stack(in_order(back(0), "x", back), axis=1), inner)
    return carried.reshape(2, DQK, DV), done, inner


def gate_rows(w_gates, core, place):
    gates = w_gates.T.reshape(2, 2, 2, OWN).transpose(1, 0, 2, 3).reshape(2, 4, OWN)
    mate = swap(gates)
    gates = jnp.where(
        core == 0,
        jnp.concatenate([gates[0], mate[0]], axis=1),
        jnp.concatenate([mate[1], gates[1]], axis=1),
    )
    gates = jnp.pad(gates.reshape(1, 4 * PIECE), ((0, 0), (0, WIDE - 4 * PIECE)))
    row = lax.broadcasted_iota(jnp.int32, (EXTRA, WIDE), 0)
    return jnp.where(row == place, gates, jnp.zeros_like(gates))


def per_device(tokens, w_query, w_key, w_value, w_gates, forget_bias, doc_lengths):
    core = lax.axis_index("core")
    y, z, x = lax.axis_index("y"), lax.axis_index("z"), lax.axis_index("x")
    chip = z * 4 + x
    last, middle = jnp.where(core == 0, x, z), jnp.where(core == 0, z, x)
    core_scalar = core[None].astype(jnp.int32)
    restore_places = jnp.concatenate([places(last), core_scalar])
    q_places = jnp.concatenate([places(middle), core_scalar])

    rest = prepare_values(core_scalar, w_value, swap(w_value))
    w_query, w_key, w_gates, rest = together(w_query, w_key, w_gates, rest)
    own = (w_query, w_key)
    mate = tuple(swap(weight) for weight in own)
    held, columns = prepare(core_scalar, own, mate, gate_rows(w_gates, core, middle * 4 + y))
    rest = lax.all_gather(rest, ("y", "z", "x"), axis=0, tiled=True)
    tokens = together(tokens[0], held)[0]
    mate_tokens = swap(tokens)

    (held,) = assemble(places(y), together(*around(held, "yy")), PIECE, False)
    held, columns = together(held, columns)
    columns = weave(q_places, together(*around(columns, "zx")), False)
    held, region = assemble(places(middle), together(*around(held, "zx")), 4 * PIECE, True)
    columns = weave(restore_places, together(*around(columns, "xz")), True)
    regions = jnp.stack(together(*around(region, "xz")))
    regions = jnp.stack([lax.dynamic_index_in_dim(regions, (j - last) % 4, 0, False) for j in range(4)])
    regions = regions[:, :, : 4 * PIECE].reshape(4, 4, 4, 4, PIECE)
    w_gates = jnp.where(
        core == 0, regions.transpose(3, 2, 1, 0, 4), regions.transpose(3, 2, 0, 1, 4)
    ).reshape(4, 4096)
    w_gates = jnp.pad(w_gates, ((0, EXTRA - 4), (0, 0)))
    gates, normed, *chunks = normalize(
        jnp.concatenate([restore_places, places(y)]), tokens, mate_tokens, w_gates
    )
    chunks, by_y = chunks[:4], chunks[4:]
    gates = gates[:4].T
    gates = gates.reshape(2, ROWS, 4)
    lengths = doc_lengths[0]
    starts = jnp.cumsum(lengths) - lengths
    shard = chip * 2 + jnp.stack([core, 1 - core])
    positions = shard[:, None] * ROWS + jnp.arange(ROWS, dtype=jnp.int32)[None, :]
    resets = jnp.any(positions[:, :, None] == starts[None, None, :], axis=-1)
    bias = lax.dynamic_slice_in_dim(forget_bias, core * 2, 2)
    in_gate = gates[:, :, :2]
    cumul = jnp.cumsum(jax.nn.log_sigmoid(gates[:, :, 2:] + bias), axis=1)
    segment = jnp.cumsum(resets.astype(jnp.int32), axis=1)
    last = cumul[:, -1]
    same = (segment == segment[:, -1:])[:, :, None]
    weight = jnp.exp(jnp.where(same, last[:, None, :] - cumul + in_gate, -1e30))
    decay = (jnp.exp(last) * (segment[:, -1:] == 0).astype(F32)).astype(BF)
    reach = jnp.exp(cumul) * (segment == 0).astype(F32)[:, :, None] * (DQK**-0.5)
    seg = segment.astype(F32)[:, :, None]
    cols = jnp.concatenate([cumul, reach, weight, seg, jnp.zeros_like(seg)], axis=2)
    rows = jnp.concatenate([cumul, in_gate, seg, jnp.zeros_like(seg), weight], axis=2)
    rows = rows.transpose(0, 2, 1)

    key = project(chunks[:1], [held])
    query = project(by_y[:1], [columns])
    held, columns, rest, key, query, cols, rows, decay = together(
        held, columns, rest, key, query, cols, rows, decay
    )
    blocks = around(held, "xz")
    columns = around(columns, "yy")
    value = jnp.dot(normed, rest, preferred_element_type=F32).astype(BF)
    key = project(chunks[1:], blocks[1:], key).astype(BF)
    state = states(cols, key, value)
    first = lax.dynamic_index_in_dim(state, core, 0, False)
    second = lax.dynamic_index_in_dim(state, 1 - core, 0, False)
    fade_first = lax.dynamic_index_in_dim(decay, core, 0, False)
    fade_second = lax.dynamic_index_in_dim(decay, 1 - core, 0, False)
    chip_state = join(fade_second, first, second)
    carried, query, inner = carry_in(
        times(fade_first, fade_second),
        chip_state,
        (
            lambda: (project(by_y[1:2], columns[1:2], query), by_y[2], by_y[3]),
            lambda done: project(done[1:], columns[2:], done[0]).astype(BF),
            lambda query: intra(cols, rows, query, key, value),
        ),
    )
    carried_second = join(fade_first, carried, first)
    mine = jnp.where(core == 0, carried, carried_second)
    other = jnp.where(core == 0, carried_second, carried)
    outgoing = readout(1, cols, query, inner, other)
    incoming = swap(outgoing)
    kept = readout(0, cols, query, inner, mine)
    result = jnp.where(
        core == 0,
        jnp.concatenate([kept, incoming], axis=1),
        jnp.concatenate([incoming, kept], axis=1),
    )
    return result.reshape(1, ROWS, 2048)


def solution(mesh):
    split = Mesh(mesh.devices.reshape(4, 4, 4, 2), ("y", "z", "x", "core"))
    weight_spec = P(("y", "z", "x", "core"), None)
    in_specs = (
        P("y", ("z", "x", "core"), None),
        weight_spec,
        weight_spec,
        weight_spec,
        weight_spec,
        P(),
        P("y", None),
    )
    out_specs = P("y", ("z", "x", "core"), None)
    return jax.shard_map(
        per_device, mesh=split, in_specs=in_specs, out_specs=out_specs, check_vma=False
    )
```

```python
import functools
import itertools

import jax
import jax.numpy as jnp
from jax import lax
from jax.experimental import pallas as pl
from jax.experimental.pallas import tpu as pltpu
from jax.sharding import Mesh, PartitionSpec as P

ROWS = 640
DQK = 256
DV = 512
OWN = 32
PIECE = 64
EXTRA = 16
WIDE = 512
BF = jnp.bfloat16
F32 = jnp.float32
COST = pl.CostEstimate(flops=0, bytes_accessed=1 << 10, transcendentals=0)
SMALL = pltpu.CompilerParams(vmem_limit_bytes=20 * 1024 * 1024)
LARGE = pltpu.CompilerParams(vmem_limit_bytes=60 * 1024 * 1024)
PARAMS = pltpu.CompilerParams(vmem_limit_bytes=20 * 1024 * 1024)


def swap(value):
    return lax.ppermute(value, "core", [(0, 1), (1, 0)])


def shift(value, axis, by):
    return lax.ppermute(value, axis, [(i, (i + by) % 4) for i in range(4)])


def hop(value, axes, by):
    names, pairs = ("y", "z", "x", "core"), []
    for source in itertools.product(range(4), range(4), range(4), range(2)):
        target = list(source)
        at = names.index(axes[source[3]])
        target[at] = (target[at] + by) % 4
        flat = [((p[0] * 4 + p[1]) * 4 + p[2]) * 2 + p[3] for p in (source, target)]
        pairs.append(tuple(flat))
    return lax.ppermute(value, names, pairs)


def around(value, axes):
    return (value,) + tuple(hop(value, axes, by) for by in (3, 2, 1))


def places(at):
    return jnp.stack([at, (at + 1) % 4, (at + 2) % 4, (at + 3) % 4]).astype(jnp.int32)


def normalize_kernel(places, own_ref, mate_ref, w_gates_ref, gates_ref, out_ref, *refs):
    chunks, by_y, scratch = refs[:4], refs[4:8], refs[8]
    raw = jnp.where(pl.program_id(0) == 0, own_ref[...], mate_ref[...])
    values = raw.astype(F32)
    scale = lax.rsqrt(jnp.mean(values * values, axis=-1, keepdims=True) + 1e-06)
    normed = (values * scale).astype(BF)
    out_ref[...] = normed
    gates_ref[...] = lax.dot_general(
        w_gates_ref[...], normed, (((1,), (1,)), ((), ())), preferred_element_type=F32
    )

    def reorder(last_step, other_step):
        for last in range(4):
            for other in range(4):
                for pair in range(2):
                    halves = []
                    for y in (2 * pair, 2 * pair + 1):
                        start = y * 1024 + last * last_step + other * other_step
                        halves.append(out_ref[:, start : start + 64])
                    start = last * 1024 + other * 256 + pair * 128
                    scratch[:, start : start + 128] = jnp.concatenate(halves, axis=1)

    pl.when(places[4] == 0)(lambda: reorder(64, 256))
    pl.when(places[4] == 1)(lambda: reorder(256, 64))
    for which in range(4):
        start = pl.multiple_of(places[which] * 1024, 1024)
        chunks[which][...] = scratch[:, pl.ds(start, 1024)]
        start = pl.multiple_of(places[5 + which] * 1024, 1024)
        by_y[which][...] = out_ref[:, pl.ds(start, 1024)]


def normalize(places, own, mate, w_gates):
    tile = 128
    steps = ROWS // tile
    return pl.pallas_call(
        normalize_kernel,
        grid_spec=pltpu.PrefetchScalarGridSpec(
            num_scalar_prefetch=1,
            grid=(2, steps),
            in_specs=[
                pl.BlockSpec((tile, 4096), lambda s, i, p: (jnp.where(s == 0, i, steps - 1), 0)),
                pl.BlockSpec((tile, 4096), lambda s, i, p: (jnp.where(s == 0, 0, i), 0)),
                pl.BlockSpec((EXTRA, 4096), lambda s, i, p: (0, 0)),
            ],
            out_specs=[pl.BlockSpec((EXTRA, tile), lambda s, i, p: (0, s * steps + i))]
            + [pl.BlockSpec((tile, 4096), lambda s, i, p: (s * steps + i, 0))]
            + [pl.BlockSpec((tile, 1024), lambda s, i, p: (s * steps + i, 0))] * 8,
            scratch_shapes=[pltpu.VMEM((tile, 4096), BF)],
        ),
        out_shape=[
            jax.ShapeDtypeStruct((EXTRA, 2 * ROWS), F32),
            jax.ShapeDtypeStruct((2 * ROWS, 4096), BF),
        ]
        + [jax.ShapeDtypeStruct((2 * ROWS, 1024), BF)] * 8,
        compiler_params=LARGE,
        cost_estimate=pl.CostEstimate(flops=0, bytes_accessed=32 << 20, transcendentals=0),
        name="normalize",
    )(places, own, mate, w_gates)


def prepare_values_kernel(core_ref, value, mate_value, rest_ref):
    core = core_ref[0]
    wide = pl.ds(pl.multiple_of(core * 2 * WIDE, WIDE), 2 * WIDE)
    for source, rows in ((value, core), (mate_value, 1 - core)):
        rest_ref[pl.ds(pl.multiple_of(rows * OWN, OWN), OWN), :] = source[:, wide]


def prepare_values(core, own, mate):
    vmem = pl.BlockSpec(memory_space=pltpu.VMEM)
    return pl.pallas_call(
        prepare_values_kernel,
        in_specs=[pl.BlockSpec(memory_space=pltpu.SMEM)] + [vmem] * 2,
        out_specs=vmem,
        out_shape=jax.ShapeDtypeStruct((PIECE, 2 * WIDE), BF),
        compiler_params=LARGE,
        cost_estimate=COST,
        name="prepare_values",
    )(core, own, mate)


def prepare_kernel(core_ref, query, key, mate_query, mate_key, region, held_ref, q_ref):
    core = core_ref[0]
    narrow = pl.ds(pl.multiple_of(core * WIDE, WIDE), WIDE)
    for queries, keys, rows in ((query, key, core), (mate_query, mate_key, 1 - core)):
        rows = pl.ds(pl.multiple_of(rows * OWN, OWN), OWN)
        q_ref[rows, :] = queries[:, narrow]
        held_ref[rows, :] = keys[:, narrow]
    held_ref[PIECE:, :] = region[...]


def prepare(core, own, mate, region):
    vmem = pl.BlockSpec(memory_space=pltpu.VMEM)
    return pl.pallas_call(
        prepare_kernel,
        in_specs=[pl.BlockSpec(memory_space=pltpu.SMEM)] + [vmem] * 5,
        out_specs=[vmem] * 2,
        out_shape=[
            jax.ShapeDtypeStruct((PIECE + EXTRA, WIDE), BF),
            jax.ShapeDtypeStruct((PIECE, WIDE), BF),
        ],
        compiler_params=LARGE,
        cost_estimate=COST,
        name="prepare",
    )(core, *own, *mate, region)


def weave_kernel(groups, places, *refs):
    blocks, out, held, sems_in, sem_out = refs[:4], *refs[4:]

    def run(target):
        copies = [
            pltpu.make_async_copy(block, target(places[which]), sems_in.at[which])
            for which, block in enumerate(blocks)
        ]
        for copy in copies:
            copy.start()
        for copy in copies:
            copy.wait()

    if groups:
        pl.when(places[4] == 0)(lambda: run(lambda place: held.at[:, place]))
        pl.when(places[4] == 1)(lambda: run(lambda place: held.at[place]))
    else:
        run(lambda place: held.at[place])
    store = pltpu.make_async_copy(held, out, sem_out)
    store.start()
    store.wait()


def weave(places, blocks, groups):
    hbm = pl.BlockSpec(memory_space=pl.ANY)
    shape = (4, 4, PIECE, WIDE) if groups else (4, PIECE, WIDE)
    blocks = [block.reshape(shape[1:]) for block in blocks]
    return pl.pallas_call(
        functools.partial(weave_kernel, groups),
        in_specs=[pl.BlockSpec(memory_space=pltpu.SMEM)] + [hbm] * 4,
        out_specs=hbm,
        out_shape=jax.ShapeDtypeStruct(shape, BF),
        scratch_shapes=[
            pltpu.VMEM(shape, BF),
            pltpu.SemaphoreType.DMA((4,)),
            pltpu.SemaphoreType.DMA,
        ],
        compiler_params=PARAMS,
        cost_estimate=COST,
        name="weave",
    )(places, *blocks).reshape(-1, WIDE)


def assemble_kernel(rows, final, places, *refs):
    blocks, out, held, regions, sems_in, sems_more, sems_out = refs[:4], refs[4:-5], *refs[-5:]
    loads, extras = [], []
    for which, block in enumerate(blocks):
        start = pl.multiple_of(places[which] * rows, PIECE)
        loads.append(
            pltpu.make_async_copy(
                block.at[pl.ds(0, rows), :], held.at[pl.ds(start, rows), :], sems_in.at[which]
            )
        )
        extras.append(
            pltpu.make_async_copy(
                block.at[pl.ds(rows, EXTRA), :], regions.at[which], sems_more.at[which]
            )
        )
    for copy in extras + loads:
        copy.start()
    for copy in extras:
        copy.wait()
    held[4 * rows :, :] = (regions[0] + regions[1]) + (regions[2] + regions[3])
    for copy in loads:
        copy.wait()
    if final:
        stores = [
            pltpu.make_async_copy(held.at[pl.ds(0, 4 * rows), :], out[0], sems_out.at[0]),
            pltpu.make_async_copy(held.at[pl.ds(4 * rows, EXTRA), :], out[1], sems_out.at[1]),
        ]
    else:
        stores = [pltpu.make_async_copy(held, out[0], sems_out.at[0])]
    for copy in stores:
        copy.start()
    for copy in stores:
        copy.wait()


def assemble(places, blocks, rows, final):
    hbm = pl.BlockSpec(memory_space=pl.ANY)
    if final:
        shapes = [(4 * rows, WIDE), (EXTRA, WIDE)]
    else:
        shapes = [(4 * rows + EXTRA, WIDE)]
    return pl.pallas_call(
        functools.partial(assemble_kernel, rows, final),
        in_specs=[pl.BlockSpec(memory_space=pltpu.SMEM)] + [hbm] * 4,
        out_specs=[hbm] * len(shapes),
        out_shape=[jax.ShapeDtypeStruct(shape, BF) for shape in shapes],
        scratch_shapes=[
            pltpu.VMEM((4 * rows + EXTRA, WIDE), BF),
            pltpu.VMEM((4, EXTRA, WIDE), BF),
            pltpu.SemaphoreType.DMA((4,)),
            pltpu.SemaphoreType.DMA((4,)),
            pltpu.SemaphoreType.DMA((2,)),
        ],
        compiler_params=PARAMS,
        cost_estimate=COST,
        name="assemble",
    )(places, *blocks)


def together(*values):
    return lax.optimization_barrier(values)


def project(chunks, weights, total=None):
    for chunk, weight in zip(chunks, weights):
        term = jnp.dot(chunk, weight, preferred_element_type=F32)
        total = term if total is None else total + term
    return total


def state_kernel(cols_ref, key_ref, left_ref, right_ref, out_ref):
    for head, value_ref in enumerate((left_ref, right_ref)):
        weight = cols_ref[0, :, 4 + head : 5 + head]
        keys = key_ref[:, head * DQK : (head + 1) * DQK]
        scaled = (keys.astype(F32) * weight).astype(BF)
        out_ref[0, head] = lax.dot_general(
            scaled, value_ref[...], (((0,), (0,)), ((), ())), preferred_element_type=F32
        ).astype(BF)


def states(cols, key, value):
    parts = [pl.BlockSpec((ROWS, WIDE), lambda s, n=n: (s, n)) for n in (0, 0, 1)]
    return pl.pallas_call(
        state_kernel,
        grid=(2,),
        in_specs=[pl.BlockSpec((1, ROWS, 8), lambda s: (s, 0, 0)), *parts],
        out_specs=pl.BlockSpec((1, 2, DQK, DV), lambda s: (s, 0, 0, 0)),
        out_shape=jax.ShapeDtypeStruct((2, 2, DQK, DV), BF),
        compiler_params=SMALL,
        cost_estimate=COST,
        name="states",
    )(cols, key, value, value)


def intra_kernel(cols_ref, rows_ref, query_ref, key_ref, left_ref, right_ref, out_ref):
    segment = cols_ref[0, :, 6:7]
    segment_row = rows_ref[0, 4:5, :]
    for head, value_ref in enumerate((left_ref, right_ref)):
        cumul = cols_ref[0, :, head : head + 1]
        cumul_row = rows_ref[0, head : head + 1, :]
        gate_row = rows_ref[0, 2 + head : 3 + head, :]
        features = slice(head * DQK, (head + 1) * DQK)
        for start, size in ((0, 256), (256, 384)):
            reach = start + size
            scores = lax.dot_general(
                query_ref[start:reach, features],
                key_ref[:reach, features],
                (((1,), (1,)), ((), ())),
                preferred_element_type=F32,
            ) * (DQK**-0.5)
            later = start + lax.broadcasted_iota(jnp.int32, (size, reach), 0)
            earlier = lax.broadcasted_iota(jnp.int32, (size, reach), 1)
            keep = (later >= earlier) & (segment[start:reach] == segment_row[:, :reach])
            diff = cumul[start:reach] - cumul_row[:, :reach] + gate_row[:, :reach]
            mixed = (scores * jnp.exp(jnp.where(keep, diff, -1e30))).astype(BF)
            out_ref[start:reach, head * DV : (head + 1) * DV] = jnp.dot(
                mixed, value_ref[:reach, :], preferred_element_type=F32
            )


def intra(cols, rows, query, key, value):
    parts = [pl.BlockSpec((ROWS, WIDE), lambda s, n=n: (s, n)) for n in (0, 0, 0, 1)]
    return pl.pallas_call(
        intra_kernel,
        grid=(2,),
        in_specs=[
            pl.BlockSpec((1, ROWS, 8), lambda s: (s, 0, 0)),
            pl.BlockSpec((1, 8, ROWS), lambda s: (s, 0, 0)),
            *parts,
        ],
        out_specs=pl.BlockSpec((ROWS, 2 * DV), lambda s: (s, 0)),
        out_shape=jax.ShapeDtypeStruct((2 * ROWS, 2 * DV), F32),
        compiler_params=SMALL,
        cost_estimate=COST,
        name="intra",
    )(cols, rows, query, key, value, value)


def readout_kernel(cols_ref, query_ref, intra_ref, carried_ref, out_ref):
    head = pl.program_id(0)
    reach = jnp.where(head == 0, cols_ref[0, :, 2:3], cols_ref[0, :, 3:4])
    between = jnp.dot(query_ref[...], carried_ref[0], preferred_element_type=F32) * reach
    readout = intra_ref[...] + between
    scale = lax.rsqrt(jnp.mean(readout * readout, axis=-1, keepdims=True) + 1e-05)
    out_ref[...] = (readout * scale).astype(BF)


def readout(slot, cols, qkv, inner, carried):
    return pl.pallas_call(
        readout_kernel,
        grid=(2,),
        in_specs=[
            pl.BlockSpec((1, ROWS, 8), lambda h: (slot, 0, 0)),
            pl.BlockSpec((ROWS, DQK), lambda h: (slot, h)),
            pl.BlockSpec((ROWS, DV), lambda h: (slot, h)),
            pl.BlockSpec((1, DQK, DV), lambda h: (h, 0, 0)),
        ],
        out_specs=pl.BlockSpec((ROWS, DV), lambda h: (0, h)),
        out_shape=jax.ShapeDtypeStruct((ROWS, 2 * DV), BF),
        compiler_params=SMALL,
        cost_estimate=COST,
        name="readout",
    )(cols, qkv, inner, carried)


def join(decay, earlier, later):
    return (decay.astype(F32)[:, None, None] * earlier.astype(F32) + later.astype(F32)).astype(BF)


def times(left, right):
    return (left.astype(F32) * right.astype(F32)).astype(BF)


def pack(state, decay):
    tail = jnp.broadcast_to(decay[:, None, None], (2, 8, DV))
    return jnp.concatenate([state, tail], axis=1)


def unpack(message):
    return message[:, :-8], message[:, -1, 0]


def in_order(mine, axis, send):
    place = lax.axis_index(axis)
    blocks = [mine] + [shift(send(by), axis, by) for by in (1, 2, 3)]
    stacked = jnp.stack(blocks)
    return [lax.dynamic_index_in_dim(stacked, (place - j) % 4, 0, False) for j in range(4)]


def carry_in(decay, state, beside):
    x, z = lax.axis_index("x"), lax.axis_index("z")
    quarters = state.reshape(2, 4, DQK // 4, DV)

    def piece(by):
        return pack(lax.dynamic_index_in_dim(quarters, (x + by) % 4, 1, False), decay)

    line = [unpack(block) for block in in_order(piece(0), "x", piece)]
    prior = jnp.zeros_like(line[0][0])
    reach = jnp.ones_like(decay)
    priors, reaches = [], []
    for block, fade in line:
        priors.append(prior)
        reaches.append(reach)
        prior = join(fade, prior, block)
        reach = times(fade, reach)
    whole, done = together(pack(prior, reach), beside[0]())
    before = jnp.zeros_like(prior)
    for j, message in enumerate(in_order(whole, "z", lambda by: whole)):
        block, fade = unpack(message)
        before = jnp.where(j < z, join(fade, before, block), before)
    backs = jnp.stack([join(reaches[j], before, priors[j]) for j in range(4)])
    backs, done = together(backs, beside[1](done))

    def back(by):
        return lax.dynamic_index_in_dim(backs, (x + by) % 4, 0, False)

    inner = beside[2](done)
    carried, inner = together(jnp.stack(in_order(back(0), "x", back), axis=1), inner)
    return carried.reshape(2, DQK, DV), done, inner


def gate_rows(w_gates, core, place):
    gates = w_gates.T.reshape(2, 2, 2, OWN).transpose(1, 0, 2, 3).reshape(2, 4, OWN)
    mate = swap(gates)
    gates = jnp.where(
        core == 0,
        jnp.concatenate([gates[0], mate[0]], axis=1),
        jnp.concatenate([mate[1], gates[1]], axis=1),
    )
    gates = jnp.pad(gates.reshape(1, 4 * PIECE), ((0, 0), (0, WIDE - 4 * PIECE)))
    row = lax.broadcasted_iota(jnp.int32, (EXTRA, WIDE), 0)
    return jnp.where(row == place, gates, jnp.zeros_like(gates))


def per_device(tokens, w_query, w_key, w_value, w_gates, forget_bias, doc_lengths):
    core = lax.axis_index("core")
    y, z, x = lax.axis_index("y"), lax.axis_index("z"), lax.axis_index("x")
    chip = z * 4 + x
    last, middle = jnp.where(core == 0, x, z), jnp.where(core == 0, z, x)
    core_scalar = core[None].astype(jnp.int32)
    restore_places = jnp.concatenate([places(last), core_scalar])
    q_places = jnp.concatenate([places(middle), core_scalar])

    rest = prepare_values(core_scalar, w_value, swap(w_value))
    w_query, w_key, w_gates, rest = together(w_query, w_key, w_gates, rest)
    own = (w_query, w_key)
    mate = tuple(swap(weight) for weight in own)
    held, columns = prepare(core_scalar, own, mate, gate_rows(w_gates, core, middle * 4 + y))
    rest = lax.all_gather(rest, ("y", "z", "x"), axis=0, tiled=True)
    tokens = together(tokens[0], held)[0]
    mate_tokens = swap(tokens)

    (held,) = assemble(places(y), together(*around(held, "yy")), PIECE, False)
    held, columns = together(held, columns)
    columns = weave(q_places, together(*around(columns, "zx")), False)
    held, region = assemble(places(middle), together(*around(held, "zx")), 4 * PIECE, True)
    columns = weave(restore_places, together(*around(columns, "xz")), True)
    regions = jnp.stack(together(*around(region, "xz")))
    regions = jnp.stack([lax.dynamic_index_in_dim(regions, (j - last) % 4, 0, False) for j in range(4)])
    regions = regions[:, :, : 4 * PIECE].reshape(4, 4, 4, 4, PIECE)
    w_gates = jnp.where(
        core == 0, regions.transpose(3, 2, 1, 0, 4), regions.transpose(3, 2, 0, 1, 4)
    ).reshape(4, 4096)
    w_gates = jnp.pad(w_gates, ((0, EXTRA - 4), (0, 0)))
    gates, normed, *chunks = normalize(
        jnp.concatenate([restore_places, places(y)]), tokens, mate_tokens, w_gates
    )
    chunks, by_y = chunks[:4], chunks[4:]
    gates = gates[:4].T
    gates = gates.reshape(2, ROWS, 4)
    lengths = doc_lengths[0]
    starts = jnp.cumsum(lengths) - lengths
    shard = chip * 2 + jnp.stack([core, 1 - core])
    positions = shard[:, None] * ROWS + jnp.arange(ROWS, dtype=jnp.int32)[None, :]
    resets = jnp.any(positions[:, :, None] == starts[None, None, :], axis=-1)
    bias = lax.dynamic_slice_in_dim(forget_bias, core * 2, 2)
    in_gate = gates[:, :, :2]
    cumul = jnp.cumsum(jax.nn.log_sigmoid(gates[:, :, 2:] + bias), axis=1)
    segment = jnp.cumsum(resets.astype(jnp.int32), axis=1)
    last = cumul[:, -1]
    same = (segment == segment[:, -1:])[:, :, None]
    weight = jnp.exp(jnp.where(same, last[:, None, :] - cumul + in_gate, -1e30))
    decay = (jnp.exp(last) * (segment[:, -1:] == 0).astype(F32)).astype(BF)
    reach = jnp.exp(cumul) * (segment == 0).astype(F32)[:, :, None] * (DQK**-0.5)
    seg = segment.astype(F32)[:, :, None]
    cols = jnp.concatenate([cumul, reach, weight, seg, jnp.zeros_like(seg)], axis=2)
    rows = jnp.concatenate([cumul, in_gate, seg, jnp.zeros_like(seg), weight], axis=2)
    rows = rows.transpose(0, 2, 1)

    key = project(chunks[:1], [held])
    held, columns, rest, key, cols, rows, decay = together(
        held, columns, rest, key, cols, rows, decay
    )
    blocks = around(held, "xz")
    columns = around(columns, "yy")
    value = jnp.dot(normed, rest, preferred_element_type=F32).astype(BF)
    key = project(chunks[1:], blocks[1:], key).astype(BF)
    state = states(cols, key, value)
    first = lax.dynamic_index_in_dim(state, core, 0, False)
    second = lax.dynamic_index_in_dim(state, 1 - core, 0, False)
    fade_first = lax.dynamic_index_in_dim(decay, core, 0, False)
    fade_second = lax.dynamic_index_in_dim(decay, 1 - core, 0, False)
    chip_state = join(fade_second, first, second)
    carried, query, inner = carry_in(
        times(fade_first, fade_second),
        chip_state,
        (
            lambda: (project(by_y[:2], columns[:2]), by_y[2], by_y[3]),
            lambda done: project(done[1:], columns[2:], done[0]).astype(BF),
            lambda query: intra(cols, rows, query, key, value),
        ),
    )
    carried_second = join(fade_first, carried, first)
    mine = jnp.where(core == 0, carried, carried_second)
    other = jnp.where(core == 0, carried_second, carried)
    outgoing = readout(1, cols, query, inner, other)
    incoming = swap(outgoing)
    kept = readout(0, cols, query, inner, mine)
    result = jnp.where(
        core == 0,
        jnp.concatenate([kept, incoming], axis=1),
        jnp.concatenate([incoming, kept], axis=1),
    )
    return result.reshape(1, ROWS, 2048)


def solution(mesh):
    split = Mesh(mesh.devices.reshape(4, 4, 4, 2), ("y", "z", "x", "core"))
    weight_spec = P(("y", "z", "x", "core"), None)
    in_specs = (
        P("y", ("z", "x", "core"), None),
        weight_spec,
        weight_spec,
        weight_spec,
        weight_spec,
        P(),
        P("y", None),
    )
    out_specs = P("y", ("z", "x", "core"), None)
    return jax.shard_map(
        per_device, mesh=split, in_specs=in_specs, out_specs=out_specs, check_vma=False
    )
```
